256 devices in a mesh: seq: 32 (over y, z), chan: 8 (over x, core).
Axes of the slice: x: 4, y: 4, z: 8, core: 2. Of those that a mesh axis runs over, the one named last changes fastest.
Arguments:
- q_branch: bfloat16 [4096, 8192], P('seq', 'chan'), may hold values from -6 to 6
- k_branch: bfloat16 [4096, 8192], P('seq', 'chan'), may hold values from -6 to 6
- v_branch: bfloat16 [4096, 8192], P('seq', 'chan'), may hold values from -6 to 6
- filter_taps: float32 [8192, 2048], P('chan', 'seq'), may hold values from -1 to 1, as said below
- out_weight: bfloat16 [8192, 8192], P('seq', 'chan'), may hold values from -0.0625 to 0.0625
- lengths: int32 [8], replicated, may hold values from 1 to 2048, 4096 in all
Outputs:
- block_output: bfloat16 [4096, 8192], P('seq', 'chan')
The draws below stay inside these ranges and needn't reach their ends.
Inputs may be any that keep to these rules, and one draw needn't show every extreme that they name: The 8 lengths add up to 4096; the longest is exactly 2048. `filter_taps`: real filter taps.
All inputs are finite; a program needn't handle non-finite values.
Results may differ from the reference program's by a relative error of at most 0.0064.
Values may be sent and summed in bfloat16 or wider, within the bound.
A program may use at most 128 MiB of HBM per device.

```python
import math
import jax
import jax.numpy as jnp
import numpy as np
from jax import lax

D = 8192
NREC = 8
TOKENS = 4096
SLOT = 2048


def draw_filter_taps(key, part):
    key = jax.random.fold_in(key, 7)
    decay_key, jitter_key = jax.random.split(key)
    mixing = jax.random.uniform(decay_key, (D, 1), jnp.float32)
    positions = jnp.arange(SLOT, dtype=jnp.float32)[None, :]
    lowest = 0.25 / SLOT
    highest = 1.0 / 30.0
    jitter = jnp.clip(jax.random.normal(jitter_key, (D, SLOT), jnp.float32), -4.0, 4.0)
    decays = jnp.exp(jnp.log(lowest) + mixing * (jnp.log(highest) - jnp.log(lowest)))
    envelope = jnp.exp(-positions * decays) * jnp.sqrt(1.0 - jnp.exp(-2.0 * decays))
    return jitter * envelope


def steps_of(rng, shape, cuts, least, high):
    factor_of = 1.0
    for dim, shards_of in cuts:
        steps = jax.random.uniform(jax.random.fold_in(jax.random.fold_in(rng, 6), dim), (shards_of,), jnp.float32, least / len(cuts), high / len(cuts))
        factor_of = factor_of * jnp.repeat(jnp.exp(steps), shape[dim] // shards_of).reshape((-1,) + (1,) * (len(shape) - 1 - dim))
    return factor_of


def split_up(number_of, total, bound, skew):
    portions = [(1 << 20) // math.isqrt(grade ** skew) + 1 for grade in range(2, number_of + 1)]
    spare, given = total - bound - (number_of - 1), [1] * (number_of - 1)
    while spare > 0:
        candidates = [i for i in range(number_of - 1) if given[i] < bound]
        pool, budget = sum([portions[i] for i in candidates]), spare
        for i in candidates:
            more = min(bound - given[i], max(1, budget * portions[i] // pool), spare)
            given[i] = given[i] + more
            spare = spare - more
    return np.array([bound] + given)


def uneven(key, amount, total, reach, lean):
    if amount == 2:
        one = jax.random.randint(key, (), max(1, total - reach), min(reach, total - 1) + 1)
        return jnp.stack([one, total - one])
    sizes = jnp.asarray(split_up(amount, total, reach, lean), jnp.int32)
    twos = (amount - 1) // 2
    giver, receiver = sizes[1:1 + 2 * twos:2], sizes[2:2 + 2 * twos:2]
    slack = jnp.minimum(giver - 1, reach - receiver)
    shifted = jax.random.randint(jax.random.fold_in(key, 1), (twos,), 0, 1 << 20) % (slack + 1)
    sizes = sizes.at[1:1 + 2 * twos:2].set(giver - shifted).at[2:2 + 2 * twos:2].set(receiver + shifted)
    return sizes[jax.random.permutation(jax.random.fold_in(key, 2), amount)]


def scatter_about(rng, extent, deviation, reach, pieces=(), held_as=jnp.bfloat16):
    values = jax.random.normal(rng, extent, jnp.float32) * deviation
    if len(pieces) > 0:
        values = steps_of(rng, extent, pieces, -0.22, 0.18) * values
    return jnp.clip(values, min=-reach, max=reach).astype(held_as)


def setup_inputs(seed: int = 0) -> dict:
    streams_of = jax.random.split(jax.random.key(seed), 7)
    return {
        "q_branch": scatter_about(streams_of[0], (TOKENS, D), 1.0, 6.0, ((0, 32), (1, 8))),
        "k_branch": scatter_about(streams_of[1], (TOKENS, D), 1.0, 6.0, ((0, 32), (1, 8))),
        "v_branch": scatter_about(streams_of[2], (TOKENS, D), 1.0, 6.0, ((0, 32), (1, 8))),
        "filter_taps": draw_filter_taps(jax.random.fold_in(streams_of[6], 71), 0),
        "out_weight": scatter_about(streams_of[4], (D, D), D ** -0.5, 0.0625, ((0, 32), (1, 8))),
        "lengths": uneven(streams_of[5], NREC, TOKENS, SLOT, 2).astype(jnp.int32),
    }


def record_tables(lengths, total, slot):
    lengths = lengths.astype(jnp.int32)
    offsets = (jnp.cumsum(lengths) - lengths).astype(jnp.int32)
    positions = jnp.arange(slot, dtype=jnp.int32)
    live = positions[None, :] < lengths[:, None]
    source = jnp.where(live, offsets[:, None] + positions[None, :], 0).reshape(-1).astype(jnp.int32)
    tokens = jnp.arange(total, dtype=jnp.int32)
    started = offsets[None, :] <= tokens[:, None]
    record = (jnp.sum(started.astype(jnp.int32), axis=1) - 1).astype(jnp.int32)
    begin = jnp.max(jnp.where(started, offsets[None, :], 0), axis=1).astype(jnp.int32)
    target = (record * slot + tokens - begin).astype(jnp.int32)
    return source, live.reshape(-1), target


def reference(q_branch, k_branch, v_branch, filter_taps, out_weight, lengths):
    product = (k_branch.astype(jnp.float32) * v_branch.astype(jnp.float32)).astype(jnp.bfloat16)
    source, live, target = record_tables(lengths, TOKENS, SLOT)
    width = min(256, D)
    blocks = D // width
    columns = product.reshape(TOKENS, blocks, width).transpose(1, 2, 0)
    filters = filter_taps.reshape(blocks, width, SLOT)

    def convolve(pair):
        stream, taps = pair
        stream = stream.astype(jnp.float32)
        slots = jnp.where(live[None, :], jnp.take(stream, source, axis=1), jnp.float32(0.0))
        slots = slots.reshape(width, NREC, SLOT)
        spectrum = jnp.fft.rfft(slots, n=2 * SLOT, axis=-1)
        response = jnp.fft.rfft(taps.astype(jnp.float32), n=2 * SLOT, axis=-1)[:, None, :]
        result = jnp.fft.irfft(spectrum * response, n=2 * SLOT, axis=-1)[..., :SLOT]
        result = result.reshape(width, NREC * SLOT)
        return jnp.take(result, target, axis=1).astype(jnp.bfloat16)

    conv_blocks = lax.map(convolve, (columns, filters))
    convolved = conv_blocks.transpose(2, 0, 1).reshape(TOKENS, D)
    gated = (q_branch.astype(jnp.float32) * convolved.astype(jnp.float32)).astype(jnp.bfloat16)
    return jnp.dot(gated, out_weight, preferred_element_type=jnp.float32).astype(jnp.bfloat16)
```

```python
import functools

import jax
import jax.numpy as jnp
import ml_dtypes
import numpy as np
from jax import lax
from jax.experimental import pallas as pl
from jax.experimental.pallas import tpu as pltpu
from jax.sharding import PartitionSpec as P

NX, NY, NZ = 4, 4, 8
NS = NY * NZ
BLK = 128
CH = 32
REC = 8
DB = 17
ROWS = 40
MESH = pl.DeviceIdType.MESH
bf16 = jnp.bfloat16
f32 = jnp.float32


def coords():
    s = lax.axis_index("seq")
    c = lax.axis_index("chan")
    return c // 2, c % 2, s // NZ, s % NZ


def dev(x, core, y, z):
    return (y * NZ + z, x * 2 + core)


def signal(sem, device):
    pl.semaphore_signal(sem, inc=1, device_id=device, device_id_type=MESH)


def remote(src, dst, send, recv, device):
    return pltpu.make_async_remote_copy(
        src_ref=src, dst_ref=dst, send_sem=send, recv_sem=recv, device_id=device, device_id_type=MESH
    )


class Ring:
    def __init__(self, wt, send, recv, x, core, y, z):
        self.wt, self.send, self.recv, self.y = wt, send, recv, y
        self.up = dev(x, core, (y + 1) % NY, z)
        self.down = dev(x, core, (y + NY - 1) % NY, z)
        self.half = wt.shape[1] // 2

    def copy(self, slot, part, k, device):
        ref = self.wt.at[slot, pl.ds(part * self.half, self.half)]
        return remote(ref, ref, self.send.at[k], self.recv.at[k], device)

    def first(self):
        y = self.y
        return [
            self.copy(y, 0, 0, self.up),
            self.copy(y, 1, 1, self.down),
            self.copy(y, 1, 2, self.up),
            self.copy(y, 0, 3, self.down),
        ]

    def forward(self):
        y = self.y
        return [
            self.copy((y + NY - 1) % NY, 0, 4, self.up),
            self.copy((y + 1) % NY, 1, 5, self.down),
        ]

    def start(self):
        for c in self.first():
            c.start()

    def pass_on(self):
        first, forward = self.first(), self.forward()
        for k in range(2):
            first[k].wait_recv()
            forward[k].start()

    def finish_recv(self):
        for c in self.first()[2:] + self.forward():
            c.wait_recv()

    def finish_send(self):
        for c in self.first() + self.forward():
            c.wait_send()


def exchange_kernel(q_ref, k_ref, v_ref, t_ref, w_ref, rx, wt, w2, tx, ssem, rsem, wsend, wrecv):
    x, core, y, z = coords()
    barrier = pltpu.get_barrier_semaphore()
    up, down = dev(x, core, (y + 1) % NY, z), dev(x, core, (y + NY - 1) % NY, z)
    signal(barrier, up)
    signal(barrier, down)

    @pl.loop(0, NS)
    def _(i):
        @pl.when(jnp.logical_not((z // 4 == core) & (i == y * NZ + z)))
        def _():
            signal(barrier, (i, x * 2 + z // 4))

    for c in range(8):
        cols = pl.ds(c * BLK, BLK)
        prod = (k_ref[:, cols].astype(f32) * v_ref[:, cols].astype(f32)).T
        tx[pl.ds(4 * c, 4), pl.ds(0, CH), :] = prod.astype(bf16).reshape(4, CH, BLK)
        gate = q_ref[:, cols].astype(f32).T
        tx[pl.ds(4 * c, 4), pl.ds(48, CH), :] = gate.astype(bf16).reshape(4, CH, BLK)
    taps = t_ref[...].reshape(NS, CH, 64)
    taps = jnp.concatenate([taps[:, :16], taps[:, 16:]], axis=2)
    tx[:, pl.ds(CH, 16), :] = taps.astype(bf16)

    own = (z // 4 == core).astype(jnp.int32)
    pl.semaphore_wait(barrier, NS - own + 2)

    def piece(i):
        p = (i + 8 * (z % 4) + 4 * core + y) % NS
        to = dev(x, (p // 4) % 2, p % 4, 4 * core + p // 8)
        here = (own == 1) & (i == 0)
        far = remote(tx.at[p], rx.at[y * NZ + z], ssem.at[i], rsem, to)
        near = pltpu.make_async_copy(tx.at[p], rx.at[y * NZ + z], rsem)
        return here, far, near

    @pl.loop(0, NS)
    def _(i):
        here, far, near = piece(i)
        pl.when(here)(near.start)
        pl.when(jnp.logical_not(here))(far.start)

    for c in range(4):
        wt[y, pl.ds(c * BLK, BLK), :] = w_ref[:, pl.ds(c * BLK, BLK)].astype(f32).T.astype(bf16)
    ring = Ring(wt, wsend, wrecv, x, core, y, z)
    ring.start()
    for c in range(4):
        w2[pl.ds(c * BLK, BLK), :] = w_ref[:, pl.ds(512 + c * BLK, BLK)].astype(f32).T.astype(bf16)
    ring.pass_on()

    @pl.loop(0, NS)
    def _(i):
        here, far, _ = piece(i)
        pl.when(jnp.logical_not(here))(far.wait_send)

    pltpu.make_async_copy(tx, rx, rsem).wait()
    ring.finish_recv()
    ring.finish_send()


def conv_kernel(len_ref, rx, fhi, flo, ihi, ilo, out, hcat, xrow, xh, gh, yh, yrow):
    lane16 = lax.broadcasted_iota(jnp.int32, (16, BLK), 1)
    lane = lax.broadcasted_iota(jnp.int32, (CH, BLK), 1)
    zero = jnp.zeros((CH, BLK), bf16)
    hcat[0, :, pl.ds(BLK, BLK)] = zero
    hcat[DB - 1, :, pl.ds(0, BLK)] = zero
    for d in range(DB - 1):
        a = rx[2 * d, pl.ds(CH, 16), :].astype(f32)
        b = rx[2 * d + 1, pl.ds(CH, 16), :].astype(f32)
        top = jnp.where(lane16 < 64, a, pltpu.roll(b, 64, 1))
        bottom = jnp.where(lane16 < 64, pltpu.roll(a, 64, 1), b)
        h = jnp.concatenate([top, bottom], axis=0).astype(bf16)
        hcat[d, :, pl.ds(0, BLK)] = h
        hcat[d + 1, :, pl.ds(BLK, BLK)] = h

    def dot(a, b):
        return jnp.dot(a, b, preferred_element_type=f32)

    taps = hcat[...].reshape(DB * CH, 2 * BLK)
    gh[...] = (dot(taps, fhi[...]) + dot(taps, flo[...])).reshape(DB, CH, 2 * BLK)

    records = []
    begin = jnp.int32(0)
    base = jnp.int32(0)
    for r in range(REC):
        end = begin + len_ref[r]
        b0 = begin // BLK
        count = (end - 1) // BLK - b0 + 1
        records.append((begin, end, b0, count, base))
        begin = end
        base = base + count

    def mask(begin, end, n):
        token = lane + n * BLK
        return (token >= begin) & (token < end)

    for begin, end, b0, count, first in records:

        @pl.loop(0, count)
        def _(i):
            row = rx[b0 + i, pl.ds(0, CH), :].astype(f32)
            xrow[first + i] = jnp.where(mask(begin, end, b0 + i), row, 0.0).astype(bf16)

    groups = (base + 7) // 8

    @pl.loop(0, groups)
    def _(g):
        rows = xrow[pl.ds(8 * g, 8)].reshape(8 * CH, BLK)
        spectrum = dot(rows, fhi[pl.ds(0, BLK), :]) + dot(rows, flo[pl.ds(0, BLK), :])
        xh[pl.ds(8 * g, 8)] = spectrum.reshape(8, CH, 2 * BLK)

    re, im = pl.ds(0, BLK), pl.ds(BLK, BLK)
    for _, _, _, count, first in records:

        @pl.loop(0, count)
        def _(i):
            def step(d, acc):
                acc_re, acc_im = acc
                xr, xi = xh[first + i - d, :, re], xh[first + i - d, :, im]
                gr, gi = gh[d, :, re], gh[d, :, im]
                return acc_re + (xr * gr - xi * gi), acc_im + (xr * gi + xi * gr)

            none = jnp.zeros((CH, BLK), f32)
            acc_re, acc_im = lax.fori_loop(0, i + 1, step, (none, none))
            yh[first + i, :, re] = acc_re
            yh[first + i, :, im] = acc_im

    @pl.loop(0, groups)
    def _(g):
        rows = yh[pl.ds(8 * g, 8)].reshape(8 * CH, 2 * BLK)
        hi = rows.astype(bf16)
        lo = (rows - hi.astype(f32)).astype(bf16)
        back = dot(hi, ihi[...]) + dot(lo, ihi[...]) + dot(hi, ilo[...])
        yrow[pl.ds(8 * g, 8)] = back.reshape(8, CH, BLK)

    for begin, end, b0, count, first in records:

        @pl.loop(0, count)
        def _(i):
            n = b0 + i
            gated = rx[n, pl.ds(48, CH), :].astype(f32) * yrow[first + i]
            out[n] = jnp.where(mask(begin, end, n), gated, out[n].astype(f32)).astype(bf16)


def project_kernel(
    g_ref, wa, w2, out, wb, gall, rbuf, sbuf, asend, arecv, bsend, brecv, csend, crecv, wsend, wrecv, zsend, zrecv
):
    x, core, y, z = coords()
    mate = dev(x, 1 - core, y, z)
    ys = [dev(x, core, (y + i) % NY, z) for i in range(1, NY)]
    xs = [dev((x + i) % NX, core, y, z) for i in range(1, NX)]
    zs = [dev(x, core, y, (z + 1) % NZ), dev(x, core, y, (z + NZ - 1) % NZ)]
    barrier = pltpu.get_barrier_semaphore()
    for d in ys + xs + zs + [mate]:
        signal(barrier, d)
    copy_w = pltpu.make_async_copy(w2, wb.at[y], wsend.at[6])
    copy_w.start()
    order = [[4], [3, 5], [2, 6], [1, 7], [0]]

    def block(rel):
        return (z + rel) % NZ

    def a_copies(rel):
        b = block(rel)
        dst = gall.at[b, x, core, pl.ds(CH * y, CH)]
        near = pltpu.make_async_copy(g_ref.at[y * NZ + b], dst, arecv.at[rel])
        far = [
            remote(g_ref.at[((y + i) % NY) * NZ + b], dst, asend.at[rel, i], arecv.at[rel], ys[i - 1])
            for i in range(1, NY)
        ]
        return near, far

    def b_copies(rel):
        ref = gall.at[block(rel), x, core]
        return [remote(ref, ref, bsend.at[rel, i], brecv.at[rel, i], xs[i - 1]) for i in range(1, NX)]

    def c_copy(rel):
        ref = gall.at[block(rel), :, core]
        return remote(ref, ref, csend.at[rel], crecv.at[rel], mate)

    pl.semaphore_wait(barrier, 9)
    for group in order:
        for rel in group:
            near, far = a_copies(rel)
            near.start()
            for c in far:
                c.start()
    copy_w.wait()
    ring = Ring(wb, wsend, wrecv, x, core, y, z)
    ring.start()
    for group in order:
        for rel in group:
            ref = gall.at[block(rel), x, core]
            pltpu.make_async_copy(ref, ref, arecv.at[rel]).wait()
            for c in b_copies(rel):
                c.start()

    def gather(step):
        for rel in order[step]:
            for c in b_copies(rel):
                c.wait_recv()
            c_copy(rel).start()
        for rel in order[step]:
            c_copy(rel).wait_recv()

    def z_copy(way, h, step):
        return remote(
            sbuf.at[way, h, step], rbuf.at[way, h, step], zsend.at[way, h, step], zrecv.at[way, h, step], zs[way]
        )

    def sends(way, h, step):
        return step < 4 and (step > 0 or way == h)

    def compute(h, step):
        w = wa if h == 0 else wb
        blocks = [block(rel) for rel in order[step]]
        ways = [h] if step == 0 else [0, 1]
        for way in ways:
            if step > 0 and sends(way, h, step - 1):
                z_copy(way, h, step - 1).wait_recv()
        for r in range(2):
            rows = pl.ds(256 * r, 256)
            acc = None
            for i in range(NX):
                sides = [gall[b, i].reshape(2 * BLK, BLK) for b in blocks]
                right = jnp.concatenate(sides, axis=1) if len(sides) > 1 else sides[0]
                term = jnp.dot(w[i, rows, :], right, preferred_element_type=f32)
                acc = term if acc is None else acc + term
            if step == 4:
                total = acc + rbuf[0, h, 3, rows, :].astype(f32) + rbuf[1, h, 3, rows, :].astype(f32)
                out[:, pl.ds(512 * h + 256 * r, 256)] = total.T.astype(bf16)
                continue
            for k, way in enumerate(ways):
                part = acc[:, k * BLK : (k + 1) * BLK]
                if step > 0 and sends(way, h, step - 1):
                    part = part + rbuf[way, h, step - 1, rows, :].astype(f32)
                sbuf[way, h, step, rows, :] = part.astype(bf16)
        if step < 4:
            for way in ways:
                z_copy(way, h, step).start()

    gather(0)
    compute(0, 0)
    ring.pass_on()
    gather(1)
    compute(0, 1)
    ring.finish_recv()
    compute(1, 0)
    gather(2)
    compute(0, 2)
    compute(1, 1)
    gather(3)
    compute(0, 3)
    compute(1, 2)
    gather(4)
    compute(0, 4)
    compute(1, 3)
    compute(1, 4)

    for rel in range(NZ):
        for c in a_copies(rel)[1] + b_copies(rel) + [c_copy(rel)]:
            c.wait_send()
    for way in range(2):
        for h in range(2):
            for step in range(4):
                if sends(way, h, step):
                    z_copy(way, h, step).wait_send()
    ring.finish_send()


def split(a):
    hi = a.astype(ml_dtypes.bfloat16)
    return hi, (a - hi.astype(np.float64)).astype(ml_dtypes.bfloat16)


def dft_tables():
    theta = 2.0 * np.pi * (np.arange(BLK) + 0.5) / (2 * BLK)
    angle = np.arange(2 * BLK)[:, None] * theta[None, :]
    sign = np.where(np.arange(2 * BLK) < BLK, 1.0, -1.0)[:, None]
    forward = sign * np.concatenate([np.cos(angle), -np.sin(angle)], axis=1)
    angle = theta[:, None] * np.arange(BLK)[None, :]
    inverse = np.concatenate([np.cos(angle), -np.sin(angle)], axis=0) / BLK
    return (*split(forward), *split(inverse))


VM = pl.BlockSpec(memory_space=pltpu.VMEM)
SM = pl.BlockSpec(memory_space=pltpu.SMEM)
shape = jax.ShapeDtypeStruct
DMA = pltpu.SemaphoreType.DMA


def conv_call(lengths, rx):
    return pl.pallas_call(
        conv_kernel,
        out_shape=shape((NS, CH, BLK), bf16),
        in_specs=[SM] + [VM] * 5,
        out_specs=VM,
        scratch_shapes=[
            pltpu.VMEM((DB, CH, 2 * BLK), bf16),
            pltpu.VMEM((ROWS, CH, BLK), bf16),
            pltpu.VMEM((ROWS, CH, 2 * BLK), f32),
            pltpu.VMEM((DB, CH, 2 * BLK), f32),
            pltpu.VMEM((ROWS, CH, 2 * BLK), f32),
            pltpu.VMEM((ROWS, CH, BLK), f32),
        ],
        compiler_params=pltpu.CompilerParams(vmem_limit_bytes=40 << 20),
        name="conv",
    )(lengths, rx, *[jnp.asarray(t) for t in dft_tables()])


def shards(q, k, v, taps, weight, lengths):
    rx, wa, w2 = pl.pallas_call(
        exchange_kernel,
        out_shape=(shape((NS, 80, BLK), bf16), shape((NY, 512, 256), bf16), shape((512, 256), bf16)),
        in_specs=[VM] * 5,
        out_specs=(VM, VM, VM),
        scratch_shapes=[
            pltpu.VMEM((NS, 80, BLK), bf16),
            DMA((NS,)),
            DMA,
            DMA((6,)),
            DMA((6,)),
        ],
        compiler_params=pltpu.CompilerParams(collective_id=0, has_side_effects=True, vmem_limit_bytes=40 << 20),
        name="exchange",
    )(q, k, v, taps, weight)
    gated = conv_call(lengths, rx)
    return pl.pallas_call(
        project_kernel,
        out_shape=shape((BLK, 1024), bf16),
        in_specs=[VM] * 3,
        out_specs=VM,
        scratch_shapes=[
            pltpu.VMEM((NY, 512, 256), bf16),
            pltpu.VMEM((NZ, NX, 2, BLK, BLK), bf16),
            pltpu.VMEM((2, 2, 4, 512, BLK), bf16),
            pltpu.VMEM((2, 2, 4, 512, BLK), bf16),
            DMA((NZ, 4)),
            DMA((NZ,)),
            DMA((NZ, 4)),
            DMA((NZ, 4)),
            DMA((NZ,)),
            DMA((NZ,)),
            DMA((7,)),
            DMA((6,)),
            DMA((2, 2, 4)),
            DMA((2, 2, 4)),
        ],
        compiler_params=pltpu.CompilerParams(collective_id=1, has_side_effects=True, vmem_limit_bytes=40 << 20),
        name="project",
    )(gated, wa, w2)


def solution(mesh):
    two = P("seq", "chan")
    in_specs = (two, two, two, P("chan", "seq"), two, P())
    return jax.shard_map(shards, mesh=mesh, in_specs=in_specs, out_specs=two, check_vma=False)
```

```python
import jax
import jax.numpy as jnp
import numpy as np
from jax import lax
from jax.experimental import pallas as pl
from jax.experimental.pallas import tpu as pltpu
from jax.sharding import PartitionSpec as P

NX, NY, NZ = 4, 4, 8
NS = NY * NZ
BLK = 128
CH = 32
REC = 8
DB = 17
MSG = 48
MESH = pl.DeviceIdType.MESH
bf16 = jnp.bfloat16
f32 = jnp.float32
ORDER = [4, 3, 5, 2, 6, 1, 7, 0]
STEPS = [[4], [3, 5], [2, 6], [1, 7], [0]]


def coords():
    s = lax.axis_index("seq")
    c = lax.axis_index("chan")
    return c // 2, c % 2, s // NZ, s % NZ


def dev(x, core, y, z):
    return (y * NZ + z, x * 2 + core)


def signal(sem, device):
    pl.semaphore_signal(sem, inc=1, device_id=device, device_id_type=MESH)


def remote(src, dst, send, recv, device):
    return pltpu.make_async_remote_copy(
        src_ref=src, dst_ref=dst, send_sem=send, recv_sem=recv, device_id=device, device_id_type=MESH
    )


def dot(a, b):
    return jnp.dot(a, b, preferred_element_type=f32)


class Ring:
    def __init__(self, wt, base, send, recv, x, core, y, z):
        self.wt, self.base, self.send, self.recv, self.y = wt, base, send, recv, y
        self.up = dev(x, core, (y + 1) % NY, z)
        self.down = dev(x, core, (y + NY - 1) % NY, z)

    def copy(self, slot, part, k, device):
        ref = self.wt.at[slot, pl.ds(self.base + part * 256, 256)]
        return remote(ref, ref, self.send.at[k], self.recv.at[k], device)

    def first(self):
        y = self.y
        return [
            self.copy(y, 0, 0, self.up),
            self.copy(y, 1, 1, self.down),
            self.copy(y, 1, 2, self.up),
            self.copy(y, 0, 3, self.down),
        ]

    def forward(self):
        y = self.y
        return [
            self.copy((y + NY - 1) % NY, 0, 4, self.up),
            self.copy((y + 1) % NY, 1, 5, self.down),
        ]

    def start(self):
        for c in self.first():
            c.start()

    def pass_on(self):
        first, forward = self.first(), self.forward()
        for k in range(2):
            first[k].wait_recv()
            forward[k].start()

    def finish_recv(self):
        for c in self.first()[2:] + self.forward():
            c.wait_recv()

    def finish_send(self):
        for c in self.first() + self.forward():
            c.wait_send()


def hyena_kernel(
    len_ref, q_hbm, k_hbm, v_hbm, t_hbm, w_hbm, tab_hbm, out,
    q_ref, k_ref, v_ref, t_ref, w_ref, tab_ref, tab, tx, rx, qt, qall, hcat, xrow, xh, gh, yh, ye, cv, wt, gall, sbuf, rbuf, seg,
    isem, ssem, rsem, qsend, qrecv, nsem, asend, arecv, bsend, brecv, csend, crecv, w0send, w0recv, w1send, w1recv,
    zsend, zrecv,
):
    x, core, y, z = coords()
    loads = [
        pltpu.make_async_copy(src, dst, isem.at[i])
        for i, (src, dst) in enumerate(
            [(k_hbm, k_ref), (v_hbm, v_ref), (t_hbm, t_ref), (w_hbm, w_ref), (q_hbm, q_ref), (tab_hbm, tab_ref)]
        )
    ]
    for c in loads:
        c.start()

    own = (z // 4 == core).astype(jnp.int32)
    mate = dev(x, 1 - core, y, z)
    ys = [dev(x, core, (y + i) % NY, z) for i in range(1, NY)]
    xs = [dev((x + i) % NX, core, y, z) for i in range(1, NX)]
    zs = [dev(x, core, y, (z + 1) % NZ), dev(x, core, y, (z + NZ - 1) % NZ)]
    barrier = pltpu.get_barrier_semaphore()
    for d in ys + xs + zs + [mate]:
        signal(barrier, d)

    @pl.loop(0, NS)
    def _(i):
        @pl.when(jnp.logical_not((own == 1) & (i == y * NZ + z)))
        def _():
            signal(barrier, (i, x * 2 + z // 4))

    loads[0].wait()
    loads[1].wait()
    for c in range(8):
        cols = pl.ds(c * BLK, BLK)
        prod = (k_ref[:, cols].astype(f32) * v_ref[:, cols].astype(f32)).T
        tx[pl.ds(4 * c, 4), pl.ds(0, CH), :] = prod.astype(bf16).reshape(4, CH, BLK)
    loads[2].wait()
    for c in range(8):
        taps = t_ref[:, pl.ds(c * BLK, BLK)].T.reshape(4, CH, 64)
        taps = jnp.concatenate([taps[:, :16], taps[:, 16:]], axis=2)
        tx[pl.ds(4 * c, 4), pl.ds(CH, 16), :] = taps.astype(bf16)

    pl.semaphore_wait(barrier, NS - own + 9)

    def piece(i):
        p = (i + 8 * (z % 4) + 4 * core + y) % NS
        to = dev(x, (p // 4) % 2, p % 4, 4 * core + p // 8)
        here = (own == 1) & (i == 0)
        src, dst = tx.at[p], rx.at[y * NZ + z]
        return here, src, dst, to

    @pl.loop(0, NS)
    def _(i):
        here, src, dst, to = piece(i)

        @pl.when(here)
        def _():
            pltpu.make_async_copy(src, dst, rsem).start()

        @pl.when(jnp.logical_not(here))
        def _():
            remote(src, dst, ssem.at[i], rsem, to).start()

    loads[3].wait()
    for c in range(4):
        wt[y, pl.ds(c * BLK, BLK), :] = w_ref[:, pl.ds(c * BLK, BLK)].astype(f32).T.astype(bf16)
    rings = [Ring(wt, 0, w0send, w0recv, x, core, y, z), Ring(wt, 512, w1send, w1recv, x, core, y, z)]
    rings[0].start()

    loads[4].wait()
    for c in range(8):
        qt[c] = q_ref[:, pl.ds(c * BLK, BLK)].astype(f32).T.astype(bf16)

    def q_piece(i):
        p = (i + 2 * (z % 4) + core) % 8
        to = dev(x, p % 2, y, 4 * core + p // 2)
        here = (own == 1) & (i == 0)
        return here, qt.at[p], qall.at[z], to

    @pl.loop(0, 8)
    def _(i):
        here, src, dst, to = q_piece(i)

        @pl.when(here)
        def _():
            pltpu.make_async_copy(src, dst, qrecv).start()

        @pl.when(jnp.logical_not(here))
        def _():
            remote(src, dst, qsend.at[i], qrecv, to).start()

    for c in range(4):
        wt[y, pl.ds(512 + c * BLK, BLK), :] = w_ref[:, pl.ds(512 + c * BLK, BLK)].astype(f32).T.astype(bf16)

    bounds = []
    begin = jnp.int32(0)
    for r in range(REC):
        bounds.append((begin, begin + len_ref[r]))
        begin = begin + len_ref[r]

    @pl.loop(0, NS)
    def _(n):
        t = n * BLK
        first, last, extra = bounds[0][0], bounds[0][1], jnp.int32(NS)
        for r in range(1, REC):
            past = bounds[r][0] <= t
            first = jnp.where(past, bounds[r][0], first)
            last = jnp.where(past, bounds[r][1], last)
            extra = jnp.where(past, NS + r, extra)
        block = first // BLK
        seg[0, n] = block
        seg[1, n] = last
        seg[2, n] = jnp.where(first == block * BLK, block, extra)

    loads[5].wait()
    for i, cols in enumerate((pl.ds(0, 2 * BLK), pl.ds(2 * BLK, BLK))):
        table = tab_ref[:, cols]
        hi = table.astype(bf16)
        lo = (table - hi.astype(f32)).astype(bf16)
        if i == 0:
            tab[0], tab[1] = hi, lo
            tab[2] = jnp.concatenate([hi[:BLK], lo[:BLK]], axis=0)
        else:
            tab[3] = jnp.concatenate([hi, lo], axis=1)
    pltpu.make_async_copy(tx, rx, rsem).wait()

    lane16 = lax.broadcasted_iota(jnp.int32, (16, BLK), 1)
    lane = lax.broadcasted_iota(jnp.int32, (CH, BLK), 1)
    zero = jnp.zeros((CH, BLK), bf16)
    hcat[0, :, pl.ds(BLK, BLK)] = zero
    hcat[DB - 1, :, pl.ds(0, BLK)] = zero

    @pl.loop(0, DB - 1)
    def _(d):
        a = rx[2 * d, pl.ds(CH, 16), :].astype(f32)
        b = rx[2 * d + 1, pl.ds(CH, 16), :].astype(f32)
        top = jnp.where(lane16 < 64, a, pltpu.roll(b, 64, 1))
        bottom = jnp.where(lane16 < 64, pltpu.roll(a, 64, 1), b)
        h = jnp.concatenate([top, bottom], axis=0).astype(bf16)
        hcat[d, :, pl.ds(0, BLK)] = h
        hcat[d + 1, :, pl.ds(BLK, BLK)] = h

    for lo, size in ((0, 8), (8, 9)):
        taps = hcat[pl.ds(lo, size)].reshape(size * CH, 2 * BLK)
        gh[pl.ds(lo, size)] = (dot(taps, tab[0]) + dot(taps, tab[1])).reshape(size, CH, 2 * BLK)

    @pl.loop(0, NS)
    def _(n):
        row = rx[n, pl.ds(0, CH), :].astype(f32)
        xrow[n] = jnp.where(lane + n * BLK < seg[1, n], row, 0.0).astype(bf16)

    xrow[NS] = zero
    for r in range(1, REC):
        begin, end = bounds[r]
        n = begin // BLK
        token = lane + n * BLK
        row = rx[n, pl.ds(0, CH), :].astype(f32)
        xrow[NS + r] = jnp.where((token >= begin) & (token < end), row, 0.0).astype(bf16)

    @pl.loop(0, 5)
    def _(g):
        rows = xrow[pl.ds(8 * g, 8)].reshape(8 * CH, BLK)
        spectrum = dot(jnp.concatenate([rows, rows], axis=1), tab[2])
        xh[pl.ds(8 * g, 8)] = spectrum.reshape(8, CH, 2 * BLK)

    re, im = pl.ds(0, BLK), pl.ds(BLK, BLK)

    def inverse(rows):
        hi = rows.astype(bf16)
        lo = (rows - hi.astype(f32)).astype(bf16)
        both = dot(hi, tab[3])
        return both[:, :BLK] + both[:, BLK:] + dot(lo, tab[3, :, :BLK])

    gr, gi = gh[0, :, re], gh[0, :, im]
    for r in range(REC):
        xr, xi = xh[NS + r, :, re], xh[NS + r, :, im]
        ye[r, :, re] = xr * gr - xi * gi
        ye[r, :, im] = xr * gi + xi * gr
    ye[:, :, re] = inverse(ye[...].reshape(REC * CH, 2 * BLK)).reshape(REC, CH, BLK)

    rings[0].pass_on()

    def place(rel):
        return (z + rel) % NZ

    def convolve(rel):
        b = place(rel)

        @pl.loop(0, NY)
        def _(j):
            n = j * NZ + b
            block, first = seg[0, n], seg[2, n]
            acc_re = jnp.zeros((CH, BLK), f32)
            acc_im = jnp.zeros((CH, BLK), f32)
            for d in range(DB):
                m = n - d
                row = jnp.where(m > block, m, jnp.where(m == block, first, NS))
                xr, xi = xh[row, :, re], xh[row, :, im]
                gr, gi = gh[d, :, re], gh[d, :, im]
                acc_re = acc_re + (xr * gr - xi * gi)
                acc_im = acc_im + (xr * gi + xi * gr)
            yh[j, :, re] = acc_re
            yh[j, :, im] = acc_im

        back = inverse(yh[...].reshape(NY * CH, 2 * BLK)).reshape(NY, CH, BLK)
        for j in range(NY):
            n = j * NZ + b
            token = lane + n * BLK
            value = back[j]
            for r in range(1, REC):
                begin, end = bounds[r]
                low = jnp.where(begin > n * BLK, begin, TOKENS_END)
                value = jnp.where((token >= low) & (token < end), ye[r, :, re], value)
            cv[rel, j] = value.astype(bf16)

    def a_dst(rel):
        return gall.at[place(rel), x, core, pl.ds(CH * y, CH)]

    def a_near(rel):
        return pltpu.make_async_copy(cv.at[rel, y], a_dst(rel), arecv.at[rel])

    def a_far(rel):
        return [
            remote(cv.at[rel, (y + i) % NY], a_dst(rel), asend.at[rel, i], arecv.at[rel], ys[i - 1])
            for i in range(1, NY)
        ]

    def b_copies(rel):
        ref = gall.at[place(rel), x, core]
        return [remote(ref, ref, bsend.at[rel, i], brecv.at[rel, i], xs[i - 1]) for i in range(1, NX)]

    def c_copy(rel):
        ref = gall.at[place(rel), :, core]
        return remote(ref, ref, csend.at[rel], crecv.at[rel], mate)

    def conv(i):
        rel = ORDER[i]
        convolve(rel)
        for c in a_far(rel):
            c.start()
        a_near(rel).start()

    def spread(i):
        rel = ORDER[i]
        b = place(rel)
        ref = gall.at[b, x, core]
        pltpu.make_async_copy(ref, ref, arecv.at[rel]).wait()
        gall[b, x, core] = (gall[b, x, core].astype(f32) * qall[b].astype(f32)).astype(bf16)
        for c in b_copies(rel):
            c.start()

    def share(i):
        rel = ORDER[i]
        for c in b_copies(rel):
            c.wait_recv()
        c_copy(rel).start()

    def ready(i):
        c_copy(ORDER[i]).wait_recv()

    def z_copy(way, h, step):
        return remote(
            sbuf.at[way, h, step], rbuf.at[way, h, step], zsend.at[way, h, step], zrecv.at[way, h, step], zs[way]
        )

    def sends(way, h, step):
        return step < 4 and (step > 0 or way == h % 2)

    def unit(h, step):
        blocks = [place(rel) for rel in STEPS[step]]
        ways = [h % 2] if step == 0 else [0, 1]
        rows = pl.ds(256 * h, 256)
        acc = None
        for i in range(NX):
            sides = [gall[b, i].reshape(2 * BLK, BLK) for b in blocks]
            right = jnp.concatenate(sides, axis=1) if len(sides) > 1 else sides[0]
            term = dot(wt[i, rows, :], right)
            acc = term if acc is None else acc + term
        for way in ways:
            if step > 0 and sends(way, h, step - 1):
                z_copy(way, h, step - 1).wait_recv()
        if step == 4:
            total = acc + rbuf[0, h, 3].astype(f32) + rbuf[1, h, 3].astype(f32)
            out[:, pl.ds(256 * h, 256)] = total.T.astype(bf16)
            return
        for i, way in enumerate(ways):
            part = acc[:, i * BLK : (i + 1) * BLK]
            if step > 0 and sends(way, h, step - 1):
                part = part + rbuf[way, h, step - 1].astype(f32)
            sbuf[way, h, step] = part.astype(bf16)
            z_copy(way, h, step).start()

    conv(0)
    conv(1)
    conv(2)
    pltpu.make_async_copy(qt, qall, qrecv).wait()
    spread(0)
    conv(3)
    spread(1)
    conv(4)
    spread(2)
    conv(5)
    spread(3)
    conv(6)
    share(0)
    spread(4)
    conv(7)
    rings[1].start()
    rings[0].finish_recv()
    ready(0)
    unit(0, 0)
    unit(1, 0)
    spread(5)
    share(1)
    share(2)
    spread(6)
    spread(7)
    ready(1)
    ready(2)
    unit(0, 1)
    unit(1, 1)
    share(3)
    share(4)
    rings[1].pass_on()
    ready(3)
    ready(4)
    unit(0, 2)
    unit(1, 2)
    rings[1].finish_recv()
    unit(2, 0)
    unit(3, 0)
    share(5)
    share(6)
    unit(2, 1)
    unit(3, 1)
    ready(5)
    ready(6)
    unit(0, 3)
    unit(1, 3)
    share(7)
    unit(2, 2)
    unit(3, 2)
    ready(7)
    unit(2, 3)
    unit(3, 3)
    for h in range(4):
        unit(h, 4)

    @pl.loop(0, NS)
    def _(i):
        here, src, dst, to = piece(i)

        @pl.when(jnp.logical_not(here))
        def _():
            remote(src, dst, ssem.at[i], rsem, to).wait_send()

    @pl.loop(0, 8)
    def _(i):
        here, src, dst, to = q_piece(i)

        @pl.when(jnp.logical_not(here))
        def _():
            remote(src, dst, qsend.at[i], qrecv, to).wait_send()

    for rel in range(NZ):
        for c in a_far(rel) + b_copies(rel) + [c_copy(rel)]:
            c.wait_send()
    for way in range(2):
        for h in range(4):
            for step in range(4):
                if sends(way, h, step):
                    z_copy(way, h, step).wait_send()
    for ring in rings:
        ring.finish_send()


TOKENS_END = NS * BLK


def dft_tables():
    theta = 2.0 * np.pi * (np.arange(BLK) + 0.5) / (2 * BLK)
    angle = np.arange(2 * BLK)[:, None] * theta[None, :]
    sign = np.where(np.arange(2 * BLK) < BLK, 1.0, -1.0)[:, None]
    forward = sign * np.concatenate([np.cos(angle), -np.sin(angle)], axis=1)
    angle = theta[:, None] * np.arange(BLK)[None, :]
    inverse = np.concatenate([np.cos(angle), -np.sin(angle)], axis=0) / BLK
    return np.concatenate([forward, inverse], axis=1).astype(np.float32)


def shards(q, k, v, taps, weight, lengths):
    vm = pl.BlockSpec(memory_space=pltpu.VMEM)
    hbm = pl.BlockSpec(memory_space=pl.ANY)
    dma = pltpu.SemaphoreType.DMA
    scratch = [
        ((BLK, 1024), bf16),
        ((BLK, 1024), bf16),
        ((BLK, 1024), bf16),
        ((64, 1024), f32),
        ((256, 1024), bf16),
        ((256, 384), f32),
        ((4, 256, 256), bf16),
        ((NS, MSG, BLK), bf16),
        ((NS, MSG, BLK), bf16),
        ((8, BLK, BLK), bf16),
        ((8, BLK, BLK), bf16),
        ((DB, CH, 2 * BLK), bf16),
        ((NS + REC, CH, BLK), bf16),
        ((NS + REC, CH, 2 * BLK), f32),
        ((DB, CH, 2 * BLK), f32),
        ((NY, CH, 2 * BLK), f32),
        ((REC, CH, 2 * BLK), f32),
        ((NZ, NY, CH, BLK), bf16),
        ((NY, 1024, 256), bf16),
        ((NZ, NX, 2, BLK, BLK), bf16),
        ((2, 4, 4, 256, BLK), bf16),
        ((2, 4, 4, 256, BLK), bf16),
    ]
    semaphores = [
        dma((6,)), dma((NS,)), dma, dma((8,)), dma, dma, dma((NZ, NY)), dma((NZ,)), dma((NZ, NX)), dma((NZ, NX)),
        dma((NZ,)), dma((NZ,)), dma((6,)), dma((6,)), dma((6,)), dma((6,)), dma((2, 4, 4)), dma((2, 4, 4)),
    ]
    return pl.pallas_call(
        hyena_kernel,
        out_shape=jax.ShapeDtypeStruct((BLK, 1024), bf16),
        in_specs=[pl.BlockSpec(memory_space=pltpu.SMEM)] + [hbm] * 6,
        out_specs=vm,
        scratch_shapes=[pltpu.VMEM(*s) for s in scratch] + [pltpu.SMEM((3, NS), jnp.int32)] + semaphores,
        compiler_params=pltpu.CompilerParams(collective_id=0, has_side_effects=True, vmem_limit_bytes=60 << 20),
        name="hyena",
    )(lengths, q, k, v, taps.T, weight, jnp.asarray(dft_tables()))


def solution(mesh):
    two = P("seq", "chan")
    in_specs = (two, two, two, P("chan", "seq"), two, P())
    return jax.shard_map(shards, mesh=mesh, in_specs=in_specs, out_specs=two, check_vma=False)
```

```python
import jax
import jax.numpy as jnp
import numpy as np
from jax import lax
from jax.experimental import pallas as pl
from jax.experimental.pallas import tpu as pltpu
from jax.sharding import PartitionSpec as P

NX, NY, NZ = 4, 4, 8
NS = NY * NZ
BLK = 128
CH = 32
REC = 8
DB = 17
MESH = pl.DeviceIdType.MESH
bf16 = jnp.bfloat16
f32 = jnp.float32
ORDER = [4, 3, 5, 2, 6, 1, 7, 0]
FAR = [2, 1, 3]
CHAINS = [(0, 0), (1, 1), (0, 1), (2, 0), (1, 2), (3, 1), (0, 2), (2, 1), (1, 3), (3, 2), (2, 2), (0, 3), (3, 3), (2, 3)]


def coords():
    s = lax.axis_index("seq")
    c = lax.axis_index("chan")
    return c // 2, c % 2, s // NZ, s % NZ


def dev(x, core, y, z):
    return (y * NZ + z, x * 2 + core)


def signal(sem, device):
    pl.semaphore_signal(sem, inc=1, device_id=device, device_id_type=MESH)


def remote(src, dst, send, recv, device):
    return pltpu.make_async_remote_copy(
        src_ref=src, dst_ref=dst, send_sem=send, recv_sem=recv, device_id=device, device_id_type=MESH
    )


def dot(a, b):
    return jnp.dot(a, b, preferred_element_type=f32)


class Ring:
    def __init__(self, wt, base, send, recv, x, core, y, z):
        self.wt, self.base, self.send, self.recv, self.y = wt, base, send, recv, y
        self.up = dev(x, core, (y + 1) % NY, z)
        self.down = dev(x, core, (y + NY - 1) % NY, z)

    def copy(self, slot, part, k, device):
        ref = self.wt.at[pl.ds(self.base + part * 256, 256), pl.ds(pl.multiple_of(slot * 256, 256), 256)]
        return remote(ref, ref, self.send.at[k], self.recv.at[k], device)

    def first(self):
        y = self.y
        return [
            self.copy(y, 0, 0, self.up),
            self.copy(y, 1, 1, self.down),
            self.copy(y, 1, 2, self.up),
            self.copy(y, 0, 3, self.down),
        ]

    def forward(self):
        y = self.y
        return [
            self.copy((y + NY - 1) % NY, 0, 4, self.up),
            self.copy((y + 1) % NY, 1, 5, self.down),
        ]

    def start(self, part):
        for c in self.first()[2 * part : 2 * part + 2]:
            c.start()

    def pass_on(self):
        first, forward = self.first(), self.forward()
        for k in range(2):
            first[k].wait_recv()
            forward[k].start()

    def finish_recv(self):
        for c in self.first()[2:] + self.forward():
            c.wait_recv()

    def finish_send(self):
        for c in self.first() + self.forward():
            c.wait_send()


def hyena_kernel(
    len_hbm, q_hbm, k_hbm, v_hbm, t_hbm, w_hbm, tab_hbm, out,
    q_ref, k_ref, v_ref, t_ref, w_ref, tab_ref, tab, tx, rx, qt, qall, hcat, xrow, xh, gh, yh, ye, cv, wt, gall, sbuf, rbuf, seg, len_ref,
    isem, ssem, rsem, qsend, qrecv, nsem, asend, arecv, bsend, brecv, csend, crecv, w0send, w0recv, w1send, w1recv,
    zsend, zrecv,
):
    x, core, y, z = coords()
    loads = [
        pltpu.make_async_copy(src, dst, isem.at[i])
        for i, (src, dst) in enumerate(
            [(k_hbm, k_ref), (v_hbm, v_ref), (t_hbm, t_ref), (w_hbm, w_ref), (q_hbm, q_ref), (tab_hbm, tab_ref), (len_hbm, len_ref)]
        )
    ]
    for c in loads:
        c.start()

    own = (z // 4 == core).astype(jnp.int32)
    mate = dev(x, 1 - core, y, z)
    ys = [dev(x, core, (y + i) % NY, z) for i in FAR]
    xs = [dev((x + i) % NX, core, y, z) for i in FAR]
    zs = [dev(x, core, y, (z + 1) % NZ), dev(x, core, y, (z + NZ - 1) % NZ)]
    barrier = pltpu.get_barrier_semaphore()
    for d in ys + xs + zs + [mate]:
        signal(barrier, d)

    @pl.loop(0, NS)
    def _(i):
        @pl.when(jnp.logical_not((own == 1) & (i == y * NZ + z)))
        def _():
            signal(barrier, (i, x * 2 + z // 4))

    loads[2].wait()
    for c in range(8):
        taps = t_ref[:, pl.ds(c * BLK, BLK)].T.reshape(4, CH, 64)
        taps = jnp.concatenate([taps[:, :16], taps[:, 16:]], axis=2)
        tx[pl.ds(4 * c, 4), pl.ds(CH, 16), :] = taps.astype(bf16)

    pl.semaphore_wait(barrier, NS - own + 9)

    def chunk(i):
        return (i + 2 * (z % 4) + core) % 8

    def piece(i):
        c = chunk(i // 4)
        yy = (y + (6 - i % 4) % 4) % NY
        to = dev(x, c % 2, yy, 4 * core + c // 2)
        here = (own == 1) & (c == 2 * (z % 4) + core) & (yy == y)
        return here, 4 * c + yy, to

    def post(i, src, dst, send, recv):
        here, p, to = piece(i)

        @pl.when(here)
        def _():
            pltpu.make_async_copy(src.at[p], dst.at[y * NZ + z], recv).start()

        @pl.when(jnp.logical_not(here))
        def _():
            remote(src.at[p], dst.at[y * NZ + z], send.at[i], recv, to).start()

    def posted(i, src, dst, send, recv):
        here, p, to = piece(i)

        @pl.when(jnp.logical_not(here))
        def _():
            remote(src.at[p], dst.at[y * NZ + z], send.at[i], recv, to).wait_send()

    for c in loads[:2]:
        c.wait()

    @pl.loop(0, 8)
    def _(i):
        c = chunk(i)
        cols = pl.ds(pl.multiple_of(c * BLK, BLK), BLK)
        prod = (k_ref[:, cols].astype(f32) * v_ref[:, cols].astype(f32)).T
        tx[pl.ds(4 * c, 4), pl.ds(0, CH), :] = prod.astype(bf16).reshape(4, CH, BLK)
        for j in range(NY):
            post(4 * i + j, tx, rx, ssem, rsem)

    loads[3].wait()
    w_cols = pl.ds(pl.multiple_of(y * 256, 256), 256)
    for c in range(4):
        wt[pl.ds(c * BLK, BLK), w_cols] = w_ref[:, pl.ds(c * BLK, BLK)].astype(f32).T.astype(bf16)
    rings = [Ring(wt, 0, w0send, w0recv, x, core, y, z), Ring(wt, 512, w1send, w1recv, x, core, y, z)]
    rings[0].start(0)
    rings[0].start(1)

    loads[4].wait()
    for c in range(8):
        qt[c] = q_ref[:, pl.ds(c * BLK, BLK)].astype(f32).T.astype(bf16)

    def q_piece(i):
        p = (i + 2 * (z % 4) + core) % 8
        to = dev(x, p % 2, y, 4 * core + p // 2)
        here = (own == 1) & (i == 0)
        return here, qt.at[p], qall.at[z], to

    @pl.loop(0, 8)
    def _(i):
        here, src, dst, to = q_piece(i)

        @pl.when(here)
        def _():
            pltpu.make_async_copy(src, dst, qrecv).start()

        @pl.when(jnp.logical_not(here))
        def _():
            remote(src, dst, qsend.at[i], qrecv, to).start()

    for c in range(4):
        wt[pl.ds(512 + c * BLK, BLK), w_cols] = w_ref[:, pl.ds(512 + c * BLK, BLK)].astype(f32).T.astype(bf16)

    loads[6].wait()
    bounds = []
    begin = jnp.int32(0)
    for r in range(REC):
        bounds.append((begin, begin + len_ref[r]))
        begin = begin + len_ref[r]

    @pl.loop(0, NS)
    def _(n):
        t = n * BLK
        first, last, extra = bounds[0][0], bounds[0][1], jnp.int32(NS)
        for r in range(1, REC):
            past = bounds[r][0] <= t
            first = jnp.where(past, bounds[r][0], first)
            last = jnp.where(past, bounds[r][1], last)
            extra = jnp.where(past, NS + r, extra)
        block = first // BLK
        seg[0, n] = block
        seg[1, n] = last
        seg[2, n] = jnp.where(first == block * BLK, block, extra)

    loads[5].wait()
    for i, cols in enumerate((pl.ds(0, 2 * BLK), pl.ds(2 * BLK, BLK))):
        table = tab_ref[:, cols]
        hi = table.astype(bf16)
        lo = (table - hi.astype(f32)).astype(bf16)
        if i == 0:
            tab[0], tab[1] = hi, lo
            tab[2] = jnp.concatenate([hi[:BLK], lo[:BLK]], axis=0)
        else:
            tab[3] = jnp.concatenate([hi, lo], axis=1)
    rings[0].pass_on()
    rings[1].start(0)
    pltpu.make_async_copy(tx, rx, rsem).wait()

    lane16 = lax.broadcasted_iota(jnp.int32, (16, BLK), 1)
    lane = lax.broadcasted_iota(jnp.int32, (CH, BLK), 1)
    zero = jnp.zeros((CH, BLK), bf16)
    hcat[0, :, pl.ds(BLK, BLK)] = zero
    hcat[DB - 1, :, pl.ds(0, BLK)] = zero

    @pl.loop(0, DB - 1)
    def _(d):
        a = rx[2 * d, pl.ds(CH, 16), :].astype(f32)
        b = rx[2 * d + 1, pl.ds(CH, 16), :].astype(f32)
        top = jnp.where(lane16 < 64, a, pltpu.roll(b, 64, 1))
        bottom = jnp.where(lane16 < 64, pltpu.roll(a, 64, 1), b)
        h = jnp.concatenate([top, bottom], axis=0).astype(bf16)
        hcat[d, :, pl.ds(0, BLK)] = h
        hcat[d + 1, :, pl.ds(BLK, BLK)] = h

    for lo, size in ((0, 8), (8, 9)):
        taps = hcat[pl.ds(lo, size)].reshape(size * CH, 2 * BLK)
        gh[pl.ds(lo, size)] = (dot(taps, tab[0]) + dot(taps, tab[1])).reshape(size, CH, 2 * BLK)

    @pl.loop(0, NS)
    def _(n):
        row = rx[n, pl.ds(0, CH), :].astype(f32)
        xrow[n] = jnp.where(lane + n * BLK < seg[1, n], row, 0.0).astype(bf16)

    xrow[NS] = zero
    for r in range(1, REC):
        begin, end = bounds[r]
        n = begin // BLK
        token = lane + n * BLK
        row = rx[n, pl.ds(0, CH), :].astype(f32)
        xrow[NS + r] = jnp.where((token >= begin) & (token < end), row, 0.0).astype(bf16)

    @pl.loop(0, 5)
    def _(g):
        rows = xrow[pl.ds(8 * g, 8)].reshape(8 * CH, BLK)
        spectrum = dot(jnp.concatenate([rows, rows], axis=1), tab[2])
        xh[pl.ds(8 * g, 8)] = spectrum.reshape(8, CH, 2 * BLK)

    re, im = pl.ds(0, BLK), pl.ds(BLK, BLK)

    def inverse(rows):
        hi = rows.astype(bf16)
        lo = (rows - hi.astype(f32)).astype(bf16)
        both = dot(hi, tab[3])
        return both[:, :BLK] + both[:, BLK:] + dot(lo, tab[3, :, :BLK])

    gr, gi = gh[0, :, re], gh[0, :, im]
    for r in range(REC):
        xr, xi = xh[NS + r, :, re], xh[NS + r, :, im]
        ye[r, :, re] = xr * gr - xi * gi
        ye[r, :, im] = xr * gi + xi * gr
    ye[:, :, re] = inverse(ye[...].reshape(REC * CH, 2 * BLK)).reshape(REC, CH, BLK)

    def place(rel):
        return (z + rel) % NZ

    def convolve(rel):
        b = place(rel)

        @pl.loop(0, NY)
        def _(j):
            n = j * NZ + b
            block, first = seg[0, n], seg[2, n]
            acc_re = jnp.zeros((CH, BLK), f32)
            acc_im = jnp.zeros((CH, BLK), f32)
            for d in range(DB):
                m = n - d
                row = jnp.where(m > block, m, jnp.where(m == block, first, NS))
                xr, xi = xh[row, :, re], xh[row, :, im]
                gr, gi = gh[d, :, re], gh[d, :, im]
                acc_re = acc_re + (xr * gr - xi * gi)
                acc_im = acc_im + (xr * gi + xi * gr)
            yh[j, :, re] = acc_re
            yh[j, :, im] = acc_im

        back = inverse(yh[...].reshape(NY * CH, 2 * BLK)).reshape(NY, CH, BLK)
        for j in range(NY):
            n = j * NZ + b
            token = lane + n * BLK
            value = back[j]
            for r in range(1, REC):
                begin, end = bounds[r]
                low = jnp.where(begin > n * BLK, begin, TOKENS_END)
                value = jnp.where((token >= low) & (token < end), ye[r, :, re], value)
            cv[rel, j] = value.astype(bf16)

    def a_dst(rel):
        return gall.at[place(rel), x, core, pl.ds(CH * y, CH)]

    def a_near(rel):
        return pltpu.make_async_copy(cv.at[rel, y], a_dst(rel), arecv.at[rel])

    def a_far(rel):
        return [
            remote(cv.at[rel, (y + i) % NY], a_dst(rel), asend.at[rel, i], arecv.at[rel], d)
            for i, d in zip(FAR, ys)
        ]

    def b_copies(rel):
        ref = gall.at[place(rel), x, core]
        return [remote(ref, ref, bsend.at[rel, i], brecv.at[rel, i], d) for i, d in enumerate(xs)]

    def c_copy(rel):
        ref = gall.at[place(rel), :, core]
        return remote(ref, ref, csend.at[rel], crecv.at[rel], mate)

    def conv(i):
        rel = ORDER[i]
        convolve(rel)
        for c in a_far(rel):
            c.start()
        a_near(rel).start()

    def spread(i):
        rel = ORDER[i]
        b = place(rel)
        ref = gall.at[b, x, core]
        pltpu.make_async_copy(ref, ref, arecv.at[rel]).wait()
        gall[b, x, core] = (gall[b, x, core].astype(f32) * qall[b].astype(f32)).astype(bf16)
        for c in b_copies(rel):
            c.start()

    def share(i):
        rel = ORDER[i]
        for c in b_copies(rel):
            c.wait_recv()
        c_copy(rel).start()

    def ready(i):
        c_copy(ORDER[i]).wait_recv()

    def z_copy(way, h, step):
        return remote(
            sbuf.at[way, h, step], rbuf.at[way, h, step], zsend.at[way, h, step], zrecv.at[way, h, step], zs[way]
        )

    def sends(way, h, step):
        return step < 4 and (step > 0 or way == h % 2)

    def rows(h):
        return pl.ds(256 * h, 256)

    def term(h, rel):
        return dot(wt[rows(h), :], gall[place(rel)].reshape(1024, BLK))

    def ring_send(h, step):
        for way in range(2):
            k = h ^ way
            total = term(k, 4 - step if way == 0 else 4 + step)
            if step > 0 and sends(way, k, step - 1):
                z_copy(way, k, step - 1).wait_recv()
                total = total + rbuf[way, k, step - 1].astype(f32)
            sbuf[way, k, step] = total.astype(bf16)
            z_copy(way, k, step).start()

    def ring_end():
        terms = [term(h, 0) for h in range(4)]
        for h in (0, 1, 2, 3):
            total = terms[h]
            for way in range(2):
                z_copy(way, h, 3).wait_recv()
                total = total + rbuf[way, h, 3].astype(f32)
            out[:, rows(h)] = total.T.astype(bf16)

    for i in range(5):
        conv(i)
    pltpu.make_async_copy(qt, qall, qrecv).wait()
    for i in range(3):
        spread(i)
        conv(5 + i)
    rings[1].start(1)
    rings[1].pass_on()
    rings[0].finish_recv()
    before = {0: ((), (0,)), 1: ((3, 4), (1, 2)), 4: ((5, 6, 7), (3, 4)), 8: ((), (5, 6))}
    for i, (h, step) in enumerate(CHAINS):
        if i == 3:
            rings[1].finish_recv()
        spreads, shares = before.get(i, ((), ()))
        for k in spreads:
            spread(k)
        for k in shares:
            share(k)
        for k in shares:
            ready(k)
        ring_send(h, step)
    share(7)
    ready(7)
    ring_end()

    @pl.loop(0, NS)
    def _(i):
        posted(i, tx, rx, ssem, rsem)

    @pl.loop(0, 8)
    def _(i):
        here, src, dst, to = q_piece(i)

        @pl.when(jnp.logical_not(here))
        def _():
            remote(src, dst, qsend.at[i], qrecv, to).wait_send()

    for rel in range(NZ):
        for c in a_far(rel) + b_copies(rel) + [c_copy(rel)]:
            c.wait_send()
    for way in range(2):
        for h in range(4):
            for step in range(4):
                if sends(way, h, step):
                    z_copy(way, h, step).wait_send()
    for ring in rings:
        ring.finish_send()


TOKENS_END = NS * BLK


def dft_tables():
    theta = 2.0 * np.pi * (np.arange(BLK) + 0.5) / (2 * BLK)
    angle = np.arange(2 * BLK)[:, None] * theta[None, :]
    sign = np.where(np.arange(2 * BLK) < BLK, 1.0, -1.0)[:, None]
    forward = sign * np.concatenate([np.cos(angle), -np.sin(angle)], axis=1)
    angle = theta[:, None] * np.arange(BLK)[None, :]
    inverse = np.concatenate([np.cos(angle), -np.sin(angle)], axis=0) / BLK
    return np.concatenate([forward, inverse], axis=1).astype(np.float32)


def shards(q, k, v, taps, weight, lengths):
    vm = pl.BlockSpec(memory_space=pltpu.VMEM)
    hbm = pl.BlockSpec(memory_space=pl.ANY)
    dma = pltpu.SemaphoreType.DMA
    scratch = [
        ((BLK, 1024), bf16),
        ((BLK, 1024), bf16),
        ((BLK, 1024), bf16),
        ((64, 1024), f32),
        ((256, 1024), bf16),
        ((256, 384), f32),
        ((4, 256, 256), bf16),
        ((NS, 48, BLK), bf16),
        ((NS, 48, BLK), bf16),
        ((8, BLK, BLK), bf16),
        ((8, BLK, BLK), bf16),
        ((DB, CH, 2 * BLK), bf16),
        ((NS + REC, CH, BLK), bf16),
        ((NS + REC, CH, 2 * BLK), f32),
        ((DB, CH, 2 * BLK), f32),
        ((NY, CH, 2 * BLK), f32),
        ((REC, CH, 2 * BLK), f32),
        ((NZ, NY, CH, BLK), bf16),
        ((1024, 1024), bf16),
        ((NZ, NX, 2, BLK, BLK), bf16),
        ((2, 4, 4, 256, BLK), bf16),
        ((2, 4, 4, 256, BLK), bf16),
    ]
    semaphores = [
        dma((7,)), dma((NS,)), dma, dma((8,)), dma, dma, dma((NZ, NY)), dma((NZ,)), dma((NZ, NX)), dma((NZ, NX)),
        dma((NZ,)), dma((NZ,)), dma((6,)), dma((6,)), dma((6,)), dma((6,)), dma((2, 4, 4)), dma((2, 4, 4)),
    ]
    return pl.pallas_call(
        hyena_kernel,
        out_shape=jax.ShapeDtypeStruct((BLK, 1024), bf16),
        in_specs=[hbm] * 7,
        out_specs=vm,
        scratch_shapes=[pltpu.VMEM(*s) for s in scratch] + [pltpu.SMEM((3, NS), jnp.int32), pltpu.SMEM((REC,), jnp.int32)] + semaphores,
        compiler_params=pltpu.CompilerParams(collective_id=0, has_side_effects=True, vmem_limit_bytes=60 << 20),
        name="hyena",
    )(lengths, q, k, v, taps.T, weight, jnp.asarray(dft_tables()))


def solution(mesh):
    two = P("seq", "chan")
    in_specs = (two, two, two, P("chan", "seq"), two, P())
    return jax.shard_map(shards, mesh=mesh, in_specs=in_specs, out_specs=two, check_vma=False)
```

```python
import jax
import jax.numpy as jnp
import numpy as np
from jax import lax
from jax.experimental import pallas as pl
from jax.experimental.pallas import tpu as pltpu
from jax.sharding import PartitionSpec as P

NX, NY, NZ = 4, 4, 8
NS = NY * NZ
BLK = 128
CH = 32
REC = 8
DB = 17
MESH = pl.DeviceIdType.MESH
bf16 = jnp.bfloat16
f32 = jnp.float32
ORDER = [4, 3, 5, 2, 6, 1, 7, 0]
FAR = [2, 1, 3]
CHAINS = [(0, 0), (1, 1), (0, 1), (2, 0), (3, 1), (1, 2), (0, 2), (2, 1), (1, 3), (3, 2), (2, 2), (0, 3), (3, 3), (2, 3)]
FARZ = ["3210", "3210", "2130", "1023", "0123", "0123", "0132", "3021"]


def coords():
    s = lax.axis_index("seq")
    c = lax.axis_index("chan")
    return c // 2, c % 2, s // NZ, s % NZ


def dev(x, core, y, z):
    return (y * NZ + z, x * 2 + core)


def signal(sem, device):
    pl.semaphore_signal(sem, inc=1, device_id=device, device_id_type=MESH)


def remote(src, dst, send, recv, device):
    return pltpu.make_async_remote_copy(
        src_ref=src, dst_ref=dst, send_sem=send, recv_sem=recv, device_id=device, device_id_type=MESH
    )


def dot(a, b):
    return jnp.dot(a, b, preferred_element_type=f32)


class Ring:
    def __init__(self, wt, base, send, recv, x, core, y, z):
        self.wt, self.base, self.send, self.recv, self.y = wt, base, send, recv, y
        self.up = dev(x, core, (y + 1) % NY, z)
        self.down = dev(x, core, (y + NY - 1) % NY, z)

    def copy(self, slot, part, k, device):
        ref = self.wt.at[pl.ds(self.base + part * 256, 256), pl.ds(pl.multiple_of(slot * 256, 256), 256)]
        return remote(ref, ref, self.send.at[k], self.recv.at[k], device)

    def first(self):
        y = self.y
        return [
            self.copy(y, 0, 0, self.up),
            self.copy(y, 1, 1, self.down),
            self.copy(y, 1, 2, self.up),
            self.copy(y, 0, 3, self.down),
        ]

    def forward(self):
        y = self.y
        return [
            self.copy((y + NY - 1) % NY, 0, 4, self.up),
            self.copy((y + 1) % NY, 1, 5, self.down),
        ]

    def start(self, part):
        for c in self.first()[2 * part : 2 * part + 2]:
            c.start()

    def pass_on(self):
        first, forward = self.first(), self.forward()
        for k in range(2):
            first[k].wait_recv()
            forward[k].start()

    def finish_recv(self):
        for c in self.first()[2:] + self.forward():
            c.wait_recv()

    def finish_send(self):
        for c in self.first() + self.forward():
            c.wait_send()


def hyena_kernel(
    len_hbm, q_hbm, k_hbm, v_hbm, t_hbm, w_hbm, tab_hbm, out,
    q_ref, k_ref, v_ref, t_ref, w_ref, tab_ref, tab, tx, rx, qt, qall, hcat, xrow, xh, gh, yh, ye, cv, wt, gall, sbuf, rbuf, result, seg, len_ref,
    isem, ssem, rsem, qsend, qrecv, nsem, asend, arecv, bsend, brecv, csend, crecv, w0send, w0recv, w1send, w1recv,
    zsend, zrecv, osem,
):
    x, core, y, z = coords()
    own = (z // 4 == core).astype(jnp.int32)
    mate = dev(x, 1 - core, y, z)
    ys = [dev(x, core, (y + i) % NY, z) for i in FAR]
    xs = [dev((x + i) % NX, core, y, z) for i in FAR]
    zs = [dev(x, core, y, (z + 1) % NZ), dev(x, core, y, (z + NZ - 1) % NZ)]
    barrier = pltpu.get_barrier_semaphore()

    @pl.loop(0, NS)
    def _(i):
        far = dev(x, z // 4, (y + 2 + i // NZ) % NY, (z + 4 + i % NZ) % NZ)

        @pl.when(jnp.logical_not((own == 1) & (i == 2 * NZ + 4)))
        def _():
            signal(barrier, far)

    for d in ys + xs + zs + [mate]:
        signal(barrier, d)

    loads = [
        pltpu.make_async_copy(src, dst, isem.at[i])
        for i, (src, dst) in enumerate(
            [(k_hbm, k_ref), (v_hbm, v_ref), (t_hbm, t_ref), (w_hbm, w_ref), (q_hbm, q_ref), (tab_hbm, tab_ref), (len_hbm, len_ref)]
        )
    ]
    for c in loads:
        c.start()

    def flip(a):
        return a.T

    loads[0].wait()
    loads[1].wait()
    for c in range(8):
        cols = pl.ds(c * BLK, BLK)
        prod = (k_ref[:, cols].astype(f32) * v_ref[:, cols].astype(f32)).astype(bf16)
        tx[pl.ds(4 * c, 4), pl.ds(0, CH), :] = flip(prod).reshape(4, CH, BLK)
    loads[2].wait()
    for c in range(8):
        taps = t_ref[:, pl.ds(c * BLK, BLK)].T.reshape(4, CH, 64)
        taps = jnp.concatenate([taps[:, :16], taps[:, 16:]], axis=2)
        tx[pl.ds(4 * c, 4), pl.ds(CH, 16), :] = taps.astype(bf16)

    pl.semaphore_wait(barrier, NS - own + 9)

    def chunk(i):
        return (i + 2 * (z % 4) + core) % 8

    def piece(i):
        c = chunk(i // 4)
        yy = (y + (6 - i % 4) % 4) % NY
        to = dev(x, c % 2, yy, 4 * core + c // 2)
        here = (own == 1) & (c == 2 * (z % 4) + core) & (yy == y)
        return here, 4 * c + yy, to

    def post(i, src, dst, send, recv):
        here, p, to = piece(i)

        @pl.when(here)
        def _():
            pltpu.make_async_copy(src.at[p], dst.at[y * NZ + z], recv).start()

        @pl.when(jnp.logical_not(here))
        def _():
            remote(src.at[p], dst.at[y * NZ + z], send.at[i], recv, to).start()

    def posted(i, src, dst, send, recv):
        here, p, to = piece(i)

        @pl.when(jnp.logical_not(here))
        def _():
            remote(src.at[p], dst.at[y * NZ + z], send.at[i], recv, to).wait_send()

    @pl.loop(0, NS)
    def _(i):
        post(i, tx, rx, ssem, rsem)

    loads[3].wait()
    w_cols = pl.ds(pl.multiple_of(y * 256, 256), 256)
    for c in range(4):
        wt[pl.ds(c * BLK, BLK), w_cols] = flip(w_ref[:, pl.ds(c * BLK, BLK)])
    rings = [Ring(wt, 0, w0send, w0recv, x, core, y, z), Ring(wt, 512, w1send, w1recv, x, core, y, z)]
    rings[0].start(0)
    rings[0].start(1)

    loads[4].wait()
    for c in range(8):
        qt[c] = flip(q_ref[:, pl.ds(c * BLK, BLK)])

    farz = jnp.int32(0)
    for i, digits in enumerate(FARZ):
        farz = jnp.where((4 * core + 8 - z) % 8 == i, int(digits[::-1], 4), farz)

    def q_piece(i):
        digit = farz
        for k in range(1, 4):
            digit = jnp.where(i // 2 == k, farz // 4**k, digit)
        p = 2 * (digit % 4) + (i + core) % 2
        to = dev(x, p % 2, y, 4 * core + p // 2)
        here = (own == 1) & (p == 2 * (z % 4) + core)
        return here, qt.at[p], qall.at[z], to

    def q_post(low, high):
        @pl.loop(low, high)
        def _(i):
            here, src, dst, to = q_piece(i)

            @pl.when(here)
            def _():
                pltpu.make_async_copy(src, dst, qrecv.at[z]).start()

            @pl.when(jnp.logical_not(here))
            def _():
                remote(src, dst, qsend.at[i], qrecv.at[z], to).start()

    q_post(0, 2)

    for c in range(4):
        wt[pl.ds(512 + c * BLK, BLK), w_cols] = flip(w_ref[:, pl.ds(512 + c * BLK, BLK)])

    loads[6].wait()
    bounds = []
    begin = jnp.int32(0)
    for r in range(REC):
        bounds.append((begin, begin + len_ref[r]))
        begin = begin + len_ref[r]

    @pl.loop(0, NS)
    def _(n):
        t = n * BLK
        first, last, extra = bounds[0][0], bounds[0][1], jnp.int32(NS)
        for r in range(1, REC):
            past = bounds[r][0] <= t
            first = jnp.where(past, bounds[r][0], first)
            last = jnp.where(past, bounds[r][1], last)
            extra = jnp.where(past, NS + r, extra)
        block = first // BLK
        seg[0, n] = block
        seg[1, n] = last
        seg[2, n] = jnp.where(first == block * BLK, block, extra)

    loads[5].wait()
    for i, cols in enumerate((pl.ds(0, 2 * BLK), pl.ds(2 * BLK, BLK))):
        table = tab_ref[:, cols]
        hi = table.astype(bf16)
        lo = (table - hi.astype(f32)).astype(bf16)
        if i == 0:
            tab[0], tab[1] = hi, lo
            tab[2] = jnp.concatenate([hi[:BLK], lo[:BLK]], axis=0)
        else:
            tab[3] = jnp.concatenate([hi, lo], axis=1)
    rings[0].pass_on()
    rings[1].start(0)
    pltpu.make_async_copy(tx, rx, rsem).wait()
    q_post(2, 8)

    lane16 = lax.broadcasted_iota(jnp.int32, (16, BLK), 1)
    lane = lax.broadcasted_iota(jnp.int32, (CH, BLK), 1)
    zero = jnp.zeros((CH, BLK), bf16)
    hcat[0, :, pl.ds(BLK, BLK)] = zero
    hcat[DB - 1, :, pl.ds(0, BLK)] = zero

    @pl.loop(0, DB - 1, unroll=4)
    def _(d):
        a = rx[2 * d, pl.ds(CH, 16), :].astype(f32)
        b = rx[2 * d + 1, pl.ds(CH, 16), :].astype(f32)
        top = jnp.where(lane16 < 64, a, pltpu.roll(b, 64, 1))
        bottom = jnp.where(lane16 < 64, pltpu.roll(a, 64, 1), b)
        h = jnp.concatenate([top, bottom], axis=0).astype(bf16)
        hcat[d, :, pl.ds(0, BLK)] = h
        hcat[d + 1, :, pl.ds(BLK, BLK)] = h

    for lo, size in ((0, 8), (8, 9)):
        taps = hcat[pl.ds(lo, size)].reshape(size * CH, 2 * BLK)
        gh[pl.ds(lo, size)] = (dot(taps, tab[0]) + dot(taps, tab[1])).reshape(size, CH, 2 * BLK)

    @pl.loop(0, NS, unroll=8)
    def _(n):
        row = rx[n, pl.ds(0, CH), :].astype(f32)
        xrow[n] = jnp.where(lane + n * BLK < seg[1, n], row, 0.0).astype(bf16)

    xrow[NS] = zero
    for r in range(1, REC):
        begin, end = bounds[r]
        n = begin // BLK
        token = lane + n * BLK
        row = rx[n, pl.ds(0, CH), :].astype(f32)
        xrow[NS + r] = jnp.where((token >= begin) & (token < end), row, 0.0).astype(bf16)

    @pl.loop(0, 5)
    def _(g):
        rows = xrow[pl.ds(8 * g, 8)].reshape(8 * CH, BLK)
        spectrum = dot(jnp.concatenate([rows, rows], axis=1), tab[2])
        xh[pl.ds(8 * g, 8)] = spectrum.reshape(8, CH, 2 * BLK)

    re, im = pl.ds(0, BLK), pl.ds(BLK, BLK)

    def inverse(rows):
        hi = rows.astype(bf16)
        lo = (rows - hi.astype(f32)).astype(bf16)
        both = dot(hi, tab[3])
        return both[:, :BLK] + both[:, BLK:] + dot(lo, tab[3, :, :BLK])

    gr, gi = gh[0, :, re], gh[0, :, im]
    for r in range(REC):
        xr, xi = xh[NS + r, :, re], xh[NS + r, :, im]
        ye[r, :, re] = xr * gr - xi * gi
        ye[r, :, im] = xr * gi + xi * gr
    ye[:, :, re] = inverse(ye[...].reshape(REC * CH, 2 * BLK)).reshape(REC, CH, BLK)

    def place(rel):
        return (z + rel) % NZ

    def convolve(rel):
        b = place(rel)

        @pl.loop(0, NY, unroll=2)
        def _(j):
            n = j * NZ + b
            block, first = seg[0, n], seg[2, n]
            acc_re = jnp.zeros((CH, BLK), f32)
            acc_im = jnp.zeros((CH, BLK), f32)
            for d in range(DB):
                m = n - d
                row = jnp.where(m > block, m, jnp.where(m == block, first, NS))
                xr, xi = xh[row, :, re], xh[row, :, im]
                gr, gi = gh[d, :, re], gh[d, :, im]
                acc_re = acc_re + (xr * gr - xi * gi)
                acc_im = acc_im + (xr * gi + xi * gr)
            yh[j, :, re] = acc_re
            yh[j, :, im] = acc_im

        back = inverse(yh[...].reshape(NY * CH, 2 * BLK)).reshape(NY, CH, BLK)
        for j in range(NY):
            n = j * NZ + b
            token = lane + n * BLK
            value = back[j]
            for r in range(1, REC):
                begin, end = bounds[r]
                low = jnp.where(begin > n * BLK, begin, TOKENS_END)
                value = jnp.where((token >= low) & (token < end), ye[r, :, re], value)
            cv[rel, j] = value.astype(bf16)

    def a_dst(rel):
        return gall.at[place(rel), x, core, pl.ds(CH * y, CH)]

    def a_near(rel):
        return pltpu.make_async_copy(cv.at[rel, y], a_dst(rel), arecv.at[rel])

    def a_far(rel):
        return [
            remote(cv.at[rel, (y + i) % NY], a_dst(rel), asend.at[rel, i], arecv.at[rel], d)
            for i, d in zip(FAR, ys)
        ]

    def b_copies(rel):
        ref = gall.at[place(rel), x, core]
        return [remote(ref, ref, bsend.at[rel, i], brecv.at[rel, i], d) for i, d in enumerate(xs)]

    def c_copy(rel):
        ref = gall.at[place(rel), :, core]
        return remote(ref, ref, csend.at[rel], crecv.at[rel], mate)

    def conv(i):
        rel = ORDER[i]
        convolve(rel)
        for c in a_far(rel):
            c.start()
        a_near(rel).start()

    def spread(i):
        rel = ORDER[i]
        b = place(rel)
        ref = gall.at[b, x, core]
        pltpu.make_async_copy(ref, ref, arecv.at[rel]).wait()
        pltpu.make_async_copy(qall.at[b], qall.at[b], qrecv.at[b]).wait()
        gall[b, x, core] = (gall[b, x, core].astype(f32) * qall[b].astype(f32)).astype(bf16)
        for c in b_copies(rel):
            c.start()

    def share(i):
        rel = ORDER[i]
        for c in b_copies(rel):
            c.wait_recv()
        c_copy(rel).start()

    def ready(i):
        c_copy(ORDER[i]).wait_recv()

    def z_copy(way, h, step):
        return remote(
            sbuf.at[way, h, step], rbuf.at[way, h, step], zsend.at[way, h, step], zrecv.at[way, h, step], zs[way]
        )

    def sends(way, h, step):
        return step < 4 and (step > 0 or way == h % 2)

    def rows(h):
        return pl.ds(256 * h, 256)

    def term(h, rel):
        return dot(wt[rows(h), :], gall[place(rel)].reshape(1024, BLK))

    def ring_send(h, step):
        for way in range(2):
            k = h ^ way
            total = term(k, 4 - step if way == 0 else 4 + step)
            if step > 0 and sends(way, k, step - 1):
                z_copy(way, k, step - 1).wait_recv()
                total = total + rbuf[way, k, step - 1].astype(f32)
            sbuf[way, k, step] = total.astype(bf16)
            z_copy(way, k, step).start()

    def store(h):
        return pltpu.make_async_copy(result.at[:, rows(h)], out.at[:, rows(h)], osem.at[h])

    def ring_end():
        terms = [term(h, 0) for h in range(4)]
        for h in (0, 1, 2, 3):
            total = terms[h]
            for way in range(2):
                z_copy(way, h, 3).wait_recv()
                total = total + rbuf[way, h, 3].astype(f32)
            result[:, rows(h)] = total.T.astype(bf16)
            store(h).start()

    for i in range(5):
        conv(i)
        if i == 2:
            rings[1].start(1)
    for i in range(3):
        spread(i)
        conv(5 + i)
    rings[1].pass_on()
    rings[0].finish_recv()
    before = {
        0: ((), (0,), (0,)),
        1: ((3, 4), (1, 2), (1, 2)),
        2: ((5, 6), (), ()),
        4: ((7,), (3, 4), ()),
        5: ((), (), (3, 4)),
        7: ((), (5, 6), ()),
        8: ((), (), (5, 6)),
        11: ((), (7,), ()),
    }
    for i, (h, step) in enumerate(CHAINS):
        if i == 3:
            rings[1].finish_recv()
        spreads, shares, needs = before.get(i, ((), (), ()))
        for k in spreads:
            spread(k)
        for k in shares:
            share(k)
        for k in needs:
            ready(k)
        ring_send(h, step)
    ready(7)
    ring_end()

    @pl.loop(0, NS)
    def _(i):
        posted(i, tx, rx, ssem, rsem)

    @pl.loop(0, 8)
    def _(i):
        here, src, dst, to = q_piece(i)

        @pl.when(jnp.logical_not(here))
        def _():
            remote(src, dst, qsend.at[i], qrecv.at[z], to).wait_send()

    for rel in range(NZ):
        for c in a_far(rel) + b_copies(rel) + [c_copy(rel)]:
            c.wait_send()
    for way in range(2):
        for h in range(4):
            for step in range(4):
                if sends(way, h, step):
                    z_copy(way, h, step).wait_send()
    for ring in rings:
        ring.finish_send()
    for h in range(4):
        store(h).wait()


TOKENS_END = NS * BLK


def dft_tables():
    theta = 2.0 * np.pi * (np.arange(BLK) + 0.5) / (2 * BLK)
    angle = np.arange(2 * BLK)[:, None] * theta[None, :]
    sign = np.where(np.arange(2 * BLK) < BLK, 1.0, -1.0)[:, None]
    forward = sign * np.concatenate([np.cos(angle), -np.sin(angle)], axis=1)
    angle = theta[:, None] * np.arange(BLK)[None, :]
    inverse = np.concatenate([np.cos(angle), -np.sin(angle)], axis=0) / BLK
    return np.concatenate([forward, inverse], axis=1).astype(np.float32)


def shards(q, k, v, taps, weight, lengths):
    hbm = pl.BlockSpec(memory_space=pl.ANY)
    dma = pltpu.SemaphoreType.DMA
    scratch = [
        ((BLK, 1024), bf16),
        ((BLK, 1024), bf16),
        ((BLK, 1024), bf16),
        ((64, 1024), f32),
        ((256, 1024), bf16),
        ((256, 384), f32),
        ((4, 256, 256), bf16),
        ((NS, 48, BLK), bf16),
        ((NS, 48, BLK), bf16),
        ((8, BLK, BLK), bf16),
        ((8, BLK, BLK), bf16),
        ((DB, CH, 2 * BLK), bf16),
        ((NS + REC, CH, BLK), bf16),
        ((NS + REC, CH, 2 * BLK), f32),
        ((DB, CH, 2 * BLK), f32),
        ((NY, CH, 2 * BLK), f32),
        ((REC, CH, 2 * BLK), f32),
        ((NZ, NY, CH, BLK), bf16),
        ((1024, 1024), bf16),
        ((NZ, NX, 2, BLK, BLK), bf16),
        ((2, 4, 4, 256, BLK), bf16),
        ((2, 4, 4, 256, BLK), bf16),
        ((BLK, 1024), bf16),
    ]
    semaphores = [
        dma((7,)), dma((NS,)), dma, dma((8,)), dma((NZ,)), dma, dma((NZ, NY)), dma((NZ,)), dma((NZ, NX)), dma((NZ, NX)),
        dma((NZ,)), dma((NZ,)), dma((6,)), dma((6,)), dma((6,)), dma((6,)), dma((2, 4, 4)), dma((2, 4, 4)), dma((4,)),
    ]
    return pl.pallas_call(
        hyena_kernel,
        out_shape=jax.ShapeDtypeStruct((BLK, 1024), bf16),
        in_specs=[hbm] * 7,
        out_specs=hbm,
        scratch_shapes=[pltpu.VMEM(*s) for s in scratch] + [pltpu.SMEM((3, NS), jnp.int32), pltpu.SMEM((REC,), jnp.int32)] + semaphores,
        compiler_params=pltpu.CompilerParams(collective_id=0, has_side_effects=True, vmem_limit_bytes=60 << 20),
        name="hyena",
    )(lengths, q, k, v, taps.T, weight, jnp.asarray(dft_tables()))


def solution(mesh):
    two = P("seq", "chan")
    in_specs = (two, two, two, P("chan", "seq"), two, P())
    return jax.shard_map(shards, mesh=mesh, in_specs=in_specs, out_specs=two, check_vma=False)
```

```python
import jax
import jax.numpy as jnp
import numpy as np
from jax import lax
from jax.experimental import pallas as pl
from jax.experimental.pallas import tpu as pltpu
from jax.sharding import PartitionSpec as P

NX, NY, NZ = 4, 4, 8
NS = NY * NZ
BLK = 128
CH = 32
REC = 8
DB = 17
MESH = pl.DeviceIdType.MESH
bf16 = jnp.bfloat16
f32 = jnp.float32
ORDER = [4, 3, 5, 2, 6, 1, 7, 0]
FAR = [2, 1, 3]
CHAINS = [(0, 0), (1, 1), (0, 1), (2, 0), (3, 1), (1, 2), (0, 2), (2, 1), (1, 3), (3, 2), (2, 2), (0, 3), (3, 3), (2, 3)]
FARZ = ["3210", "3210", "2130", "1023", "0123", "0123", "0132", "3021"]


def coords():
    s = lax.axis_index("seq")
    c = lax.axis_index("chan")
    return c // 2, c % 2, s // NZ, s % NZ


def dev(x, core, y, z):
    return (y * NZ + z, x * 2 + core)


def signal(sem, device):
    pl.semaphore_signal(sem, inc=1, device_id=device, device_id_type=MESH)


def remote(src, dst, send, recv, device):
    return pltpu.make_async_remote_copy(
        src_ref=src, dst_ref=dst, send_sem=send, recv_sem=recv, device_id=device, device_id_type=MESH
    )


def dot(a, b):
    return jnp.dot(a, b, preferred_element_type=f32)


class Ring:
    def __init__(self, wt, base, send, recv, x, core, y, z):
        self.wt, self.base, self.send, self.recv, self.y = wt, base, send, recv, y
        self.up = dev(x, core, (y + 1) % NY, z)
        self.down = dev(x, core, (y + NY - 1) % NY, z)

    def copy(self, slot, part, k, device):
        ref = self.wt.at[pl.ds(self.base + part * 256, 256), pl.ds(pl.multiple_of(slot * 256, 256), 256)]
        return remote(ref, ref, self.send.at[k], self.recv.at[k], device)

    def first(self):
        y = self.y
        return [
            self.copy(y, 0, 0, self.up),
            self.copy(y, 1, 1, self.down),
            self.copy(y, 1, 2, self.up),
            self.copy(y, 0, 3, self.down),
        ]

    def forward(self):
        y = self.y
        return [
            self.copy((y + NY - 1) % NY, 0, 4, self.up),
            self.copy((y + 1) % NY, 1, 5, self.down),
        ]

    def start(self, part):
        for c in self.first()[2 * part : 2 * part + 2]:
            c.start()

    def pass_on(self):
        first, forward = self.first(), self.forward()
        for k in range(2):
            first[k].wait_recv()
            forward[k].start()

    def finish_recv(self):
        for c in self.first()[2:] + self.forward():
            c.wait_recv()

    def finish_send(self):
        for c in self.first() + self.forward():
            c.wait_send()


def hyena_kernel(
    len_hbm, q_hbm, k_hbm, v_hbm, t_hbm, w_hbm, tab_hbm, out,
    q_ref, k_ref, v_ref, t_ref, w_ref, tab_ref, tab, tx, rx, qt, qall, hcat, xh, gh, yh, ye, cv, wt, gall, sbuf, rbuf, result, seg, len_ref,
    isem, ssem, rsem, qsend, qrecv, nsem, asend, arecv, bsend, brecv, csend, crecv, w0send, w0recv, w1send, w1recv,
    zsend, zrecv, osem,
):
    x, core, y, z = coords()
    own = (z // 4 == core).astype(jnp.int32)
    mate = dev(x, 1 - core, y, z)
    ys = [dev(x, core, (y + i) % NY, z) for i in FAR]
    xs = [dev((x + i) % NX, core, y, z) for i in FAR]
    zs = [dev(x, core, y, (z + 1) % NZ), dev(x, core, y, (z + NZ - 1) % NZ)]
    barrier = pltpu.get_barrier_semaphore()

    @pl.loop(0, NS)
    def _(i):
        far = dev(x, z // 4, (y + 2 + i // NZ) % NY, (z + 4 + i % NZ) % NZ)

        @pl.when(jnp.logical_not((own == 1) & (i == 2 * NZ + 4)))
        def _():
            signal(barrier, far)

    for d in ys + xs + zs + [mate]:
        signal(barrier, d)

    loads = [
        pltpu.make_async_copy(src, dst, isem.at[i])
        for i, (src, dst) in enumerate(
            [(k_hbm, k_ref), (v_hbm, v_ref), (t_hbm, t_ref), (w_hbm, w_ref), (q_hbm, q_ref), (tab_hbm, tab_ref), (len_hbm, len_ref)]
        )
    ]
    for c in loads:
        c.start()

    def flip(a):
        return a.T

    loads[0].wait()
    loads[1].wait()
    for c in range(8):
        cols = pl.ds(c * BLK, BLK)
        prod = (k_ref[:, cols].astype(f32) * v_ref[:, cols].astype(f32)).astype(bf16)
        tx[pl.ds(4 * c, 4), pl.ds(0, CH), :] = flip(prod).reshape(4, CH, BLK)
    loads[2].wait()
    for c in range(8):
        taps = t_ref[:, pl.ds(c * BLK, BLK)].T.reshape(4, CH, 64)
        taps = jnp.concatenate([taps[:, :16], taps[:, 16:]], axis=2)
        tx[pl.ds(4 * c, 4), pl.ds(CH, 16), :] = taps.astype(bf16)

    pl.semaphore_wait(barrier, NS - own + 9)

    def chunk(i):
        return (i + 2 * (z % 4) + core) % 8

    def piece(i):
        c = chunk(i // 4)
        yy = (y + (6 - i % 4) % 4) % NY
        to = dev(x, c % 2, yy, 4 * core + c // 2)
        here = (own == 1) & (c == 2 * (z % 4) + core) & (yy == y)
        return here, 4 * c + yy, to

    def post(i, src, dst, send, recv):
        here, p, to = piece(i)

        @pl.when(here)
        def _():
            pltpu.make_async_copy(src.at[p], dst.at[y * NZ + z], recv).start()

        @pl.when(jnp.logical_not(here))
        def _():
            remote(src.at[p], dst.at[y * NZ + z], send.at[i], recv, to).start()

    def posted(i, src, dst, send, recv):
        here, p, to = piece(i)

        @pl.when(jnp.logical_not(here))
        def _():
            remote(src.at[p], dst.at[y * NZ + z], send.at[i], recv, to).wait_send()

    @pl.loop(0, NS)
    def _(i):
        post(i, tx, rx, ssem, rsem)

    loads[3].wait()
    w_cols = pl.ds(pl.multiple_of(y * 256, 256), 256)
    for c in range(4):
        wt[pl.ds(c * BLK, BLK), w_cols] = flip(w_ref[:, pl.ds(c * BLK, BLK)])
    rings = [Ring(wt, 0, w0send, w0recv, x, core, y, z), Ring(wt, 512, w1send, w1recv, x, core, y, z)]
    rings[0].start(0)
    rings[0].start(1)

    loads[4].wait()
    for c in range(8):
        qt[c] = flip(q_ref[:, pl.ds(c * BLK, BLK)])

    farz = jnp.int32(0)
    for i, digits in enumerate(FARZ):
        farz = jnp.where((4 * core + 8 - z) % 8 == i, int(digits[::-1], 4), farz)

    def q_piece(i):
        digit = farz
        for k in range(1, 4):
            digit = jnp.where(i // 2 == k, farz // 4**k, digit)
        p = 2 * (digit % 4) + (i + core) % 2
        to = dev(x, p % 2, y, 4 * core + p // 2)
        here = (own == 1) & (p == 2 * (z % 4) + core)
        return here, qt.at[p], qall.at[z], to

    def q_post(low, high):
        @pl.loop(low, high)
        def _(i):
            here, src, dst, to = q_piece(i)

            @pl.when(here)
            def _():
                pltpu.make_async_copy(src, dst, qrecv.at[z]).start()

            @pl.when(jnp.logical_not(here))
            def _():
                remote(src, dst, qsend.at[i], qrecv.at[z], to).start()

    q_post(0, 2)

    for c in range(4):
        wt[pl.ds(512 + c * BLK, BLK), w_cols] = flip(w_ref[:, pl.ds(512 + c * BLK, BLK)])

    loads[6].wait()
    bounds = []
    begin = jnp.int32(0)
    for r in range(REC):
        bounds.append((begin, begin + len_ref[r]))
        begin = begin + len_ref[r]

    @pl.loop(0, NS)
    def _(n):
        t = n * BLK
        first, last, extra = bounds[0][0], bounds[0][1], jnp.int32(NS)
        for r in range(1, REC):
            past = bounds[r][0] <= t
            first = jnp.where(past, bounds[r][0], first)
            last = jnp.where(past, bounds[r][1], last)
            extra = jnp.where(past, NS + r, extra)
        block = first // BLK
        seg[0, n] = block
        seg[1, n] = last
        seg[2, n] = jnp.where(first == block * BLK, block, extra)

    loads[5].wait()
    for i, cols in enumerate((pl.ds(0, 2 * BLK), pl.ds(2 * BLK, BLK))):
        table = tab_ref[:, cols]
        hi = table.astype(bf16)
        lo = (table - hi.astype(f32)).astype(bf16)
        if i == 0:
            tab[0], tab[1] = hi, lo
            tab[2] = jnp.concatenate([hi[:BLK], lo[:BLK]], axis=0)
        else:
            tab[3] = jnp.concatenate([hi, lo], axis=1)
    rings[0].pass_on()
    rings[1].start(0)
    pltpu.make_async_copy(tx, rx, rsem).wait()
    q_post(2, 8)

    lane16 = lax.broadcasted_iota(jnp.int32, (16, BLK), 1)
    lane = lax.broadcasted_iota(jnp.int32, (CH, BLK), 1)
    zero = jnp.zeros((CH, BLK), bf16)
    hcat[0, :, pl.ds(BLK, BLK)] = zero
    hcat[DB - 1, :, pl.ds(0, BLK)] = zero

    for d in range(DB - 1):
        a = rx[2 * d, pl.ds(CH, 16), :].astype(f32)
        b = rx[2 * d + 1, pl.ds(CH, 16), :].astype(f32)
        top = jnp.where(lane16 < 64, a, pltpu.roll(b, 64, 1))
        bottom = jnp.where(lane16 < 64, pltpu.roll(a, 64, 1), b)
        h = jnp.concatenate([top, bottom], axis=0).astype(bf16)
        hcat[d, :, pl.ds(0, BLK)] = h
        hcat[d + 1, :, pl.ds(BLK, BLK)] = h

    def row(n):
        if n < NS:
            value = rx[n, pl.ds(0, CH), :].astype(f32)
            return jnp.where(lane + n * BLK < seg[1, n], value, 0.0).astype(bf16)
        if n == NS:
            return zero
        begin, end = bounds[n - NS]
        m = begin // BLK
        token = lane + m * BLK
        value = rx[m, pl.ds(0, CH), :].astype(f32)
        return jnp.where((token >= begin) & (token < end), value, 0.0).astype(bf16)

    for g in range(5):
        rows = jnp.concatenate([row(8 * g + n) for n in range(8)], axis=0)
        spectrum = dot(jnp.concatenate([rows, rows], axis=1), tab[2])
        xh[pl.ds(8 * g, 8)] = spectrum.reshape(8, CH, 2 * BLK)

    for lo, size in ((0, 8), (8, 9)):
        taps = hcat[pl.ds(lo, size)].reshape(size * CH, 2 * BLK)
        gh[pl.ds(lo, size)] = (dot(taps, tab[0]) + dot(taps, tab[1])).reshape(size, CH, 2 * BLK)

    re, im = pl.ds(0, BLK), pl.ds(BLK, BLK)

    def inverse(rows):
        hi = rows.astype(bf16)
        lo = (rows - hi.astype(f32)).astype(bf16)
        both = dot(hi, tab[3])
        return both[:, :BLK] + both[:, BLK:] + dot(lo, tab[3, :, :BLK])

    gr, gi = gh[0, :, re], gh[0, :, im]
    for r in range(REC):
        xr, xi = xh[NS + r, :, re], xh[NS + r, :, im]
        ye[r, :, re] = xr * gr - xi * gi
        ye[r, :, im] = xr * gi + xi * gr
    ye[:, :, re] = inverse(ye[...].reshape(REC * CH, 2 * BLK)).reshape(REC, CH, BLK)

    def place(rel):
        return (z + rel) % NZ

    def convolve(rel):
        b = place(rel)

        @pl.loop(0, NY, unroll=4)
        def _(j):
            n = j * NZ + b
            block, first = seg[0, n], seg[2, n]
            acc_re = jnp.zeros((CH, BLK), f32)
            acc_im = jnp.zeros((CH, BLK), f32)
            for d in range(DB):
                m = n - d
                row = jnp.where(m > block, m, jnp.where(m == block, first, NS))
                xr, xi = xh[row, :, re], xh[row, :, im]
                gr, gi = gh[d, :, re], gh[d, :, im]
                acc_re = acc_re + (xr * gr - xi * gi)
                acc_im = acc_im + (xr * gi + xi * gr)
            yh[j, :, re] = acc_re
            yh[j, :, im] = acc_im

        back = inverse(yh[...].reshape(NY * CH, 2 * BLK)).reshape(NY, CH, BLK)
        for j in range(NY):
            n = j * NZ + b
            token = lane + n * BLK
            value = back[j]
            for r in range(1, REC):
                begin, end = bounds[r]
                low = jnp.where(begin > n * BLK, begin, TOKENS_END)
                value = jnp.where((token >= low) & (token < end), ye[r, :, re], value)
            cv[rel, j] = value.astype(bf16)

    def a_dst(rel):
        return gall.at[place(rel), x, core, pl.ds(CH * y, CH)]

    def a_near(rel):
        return pltpu.make_async_copy(cv.at[rel, y], a_dst(rel), arecv.at[rel])

    def a_far(rel):
        return [
            remote(cv.at[rel, (y + i) % NY], a_dst(rel), asend.at[rel, i], arecv.at[rel], d)
            for i, d in zip(FAR, ys)
        ]

    def b_copies(rel):
        ref = gall.at[place(rel), x, core]
        return [remote(ref, ref, bsend.at[rel, i], brecv.at[rel, i], d) for i, d in enumerate(xs)]

    def c_copy(rel):
        ref = gall.at[place(rel), :, core]
        return remote(ref, ref, csend.at[rel], crecv.at[rel], mate)

    def conv(i):
        rel = ORDER[i]
        convolve(rel)
        for c in a_far(rel):
            c.start()
        a_near(rel).start()

    def spread(i):
        rel = ORDER[i]
        b = place(rel)
        ref = gall.at[b, x, core]
        pltpu.make_async_copy(ref, ref, arecv.at[rel]).wait()
        pltpu.make_async_copy(qall.at[b], qall.at[b], qrecv.at[b]).wait()
        gall[b, x, core] = (gall[b, x, core].astype(f32) * qall[b].astype(f32)).astype(bf16)
        for c in b_copies(rel):
            c.start()

    def share(i):
        rel = ORDER[i]
        for c in b_copies(rel):
            c.wait_recv()
        c_copy(rel).start()

    def ready(i):
        c_copy(ORDER[i]).wait_recv()

    def z_copy(way, h, step):
        return remote(
            sbuf.at[way, h, step], rbuf.at[way, h, step], zsend.at[way, h, step], zrecv.at[way, h, step], zs[way]
        )

    def sends(way, h, step):
        return step < 4 and (step > 0 or way == h % 2)

    def rows(h):
        return pl.ds(256 * h, 256)

    def term(h, rel):
        return dot(wt[rows(h), :], gall[place(rel)].reshape(1024, BLK))

    def ring_send(h, step):
        for way in range(2):
            k = h ^ way
            total = term(k, 4 - step if way == 0 else 4 + step)
            if step > 0 and sends(way, k, step - 1):
                z_copy(way, k, step - 1).wait_recv()
                total = total + rbuf[way, k, step - 1].astype(f32)
            sbuf[way, k, step] = total.astype(bf16)
            z_copy(way, k, step).start()

    def store(h):
        return pltpu.make_async_copy(result.at[:, rows(h)], out.at[:, rows(h)], osem.at[h])

    def ring_end():
        terms = [term(h, 0) for h in range(4)]
        for h in (0, 1, 2, 3):
            total = terms[h]
            for way in range(2):
                z_copy(way, h, 3).wait_recv()
                total = total + rbuf[way, h, 3].astype(f32)
            result[:, rows(h)] = total.T.astype(bf16)
            store(h).start()

    for i in range(4):
        conv(i)
        if i == 2:
            rings[1].start(1)
    for i in range(4):
        if i < 3:
            spread(i)
        conv(4 + i)
    rings[1].pass_on()
    rings[0].finish_recv()
    before = {
        0: ((), (0,), (0,)),
        1: ((3, 4), (1, 2), (1, 2)),
        2: ((5, 6), (), ()),
        4: ((7,), (3, 4), ()),
        5: ((), (), (3, 4)),
        7: ((), (5, 6), ()),
        8: ((), (), (5, 6)),
        11: ((), (7,), ()),
    }
    for i, (h, step) in enumerate(CHAINS):
        if i == 3:
            rings[1].finish_recv()
        spreads, shares, needs = before.get(i, ((), (), ()))
        for k in spreads:
            spread(k)
        for k in shares:
            share(k)
        for k in needs:
            ready(k)
        ring_send(h, step)
    ready(7)
    ring_end()

    @pl.loop(0, NS)
    def _(i):
        posted(i, tx, rx, ssem, rsem)

    @pl.loop(0, 8)
    def _(i):
        here, src, dst, to = q_piece(i)

        @pl.when(jnp.logical_not(here))
        def _():
            remote(src, dst, qsend.at[i], qrecv.at[z], to).wait_send()

    for rel in range(NZ):
        for c in a_far(rel) + b_copies(rel) + [c_copy(rel)]:
            c.wait_send()
    for way in range(2):
        for h in range(4):
            for step in range(4):
                if sends(way, h, step):
                    z_copy(way, h, step).wait_send()
    for ring in rings:
        ring.finish_send()
    for h in range(4):
        store(h).wait()


TOKENS_END = NS * BLK


def dft_tables():
    theta = 2.0 * np.pi * (np.arange(BLK) + 0.5) / (2 * BLK)
    angle = np.arange(2 * BLK)[:, None] * theta[None, :]
    sign = np.where(np.arange(2 * BLK) < BLK, 1.0, -1.0)[:, None]
    forward = sign * np.concatenate([np.cos(angle), -np.sin(angle)], axis=1)
    angle = theta[:, None] * np.arange(BLK)[None, :]
    inverse = np.concatenate([np.cos(angle), -np.sin(angle)], axis=0) / BLK
    return np.concatenate([forward, inverse], axis=1).astype(np.float32)


def shards(q, k, v, taps, weight, lengths):
    hbm = pl.BlockSpec(memory_space=pl.ANY)
    dma = pltpu.SemaphoreType.DMA
    scratch = [
        ((BLK, 1024), bf16),
        ((BLK, 1024), bf16),
        ((BLK, 1024), bf16),
        ((64, 1024), f32),
        ((256, 1024), bf16),
        ((256, 384), f32),
        ((4, 256, 256), bf16),
        ((NS, 48, BLK), bf16),
        ((NS, 48, BLK), bf16),
        ((8, BLK, BLK), bf16),
        ((8, BLK, BLK), bf16),
        ((DB, CH, 2 * BLK), bf16),
        ((NS + REC, CH, 2 * BLK), f32),
        ((DB, CH, 2 * BLK), f32),
        ((NY, CH, 2 * BLK), f32),
        ((REC, CH, 2 * BLK), f32),
        ((NZ, NY, CH, BLK), bf16),
        ((1024, 1024), bf16),
        ((NZ, NX, 2, BLK, BLK), bf16),
        ((2, 4, 4, 256, BLK), bf16),
        ((2, 4, 4, 256, BLK), bf16),
        ((BLK, 1024), bf16),
    ]
    semaphores = [
        dma((7,)), dma((NS,)), dma, dma((8,)), dma((NZ,)), dma, dma((NZ, NY)), dma((NZ,)), dma((NZ, NX)), dma((NZ, NX)),
        dma((NZ,)), dma((NZ,)), dma((6,)), dma((6,)), dma((6,)), dma((6,)), dma((2, 4, 4)), dma((2, 4, 4)), dma((4,)),
    ]
    return pl.pallas_call(
        hyena_kernel,
        out_shape=jax.ShapeDtypeStruct((BLK, 1024), bf16),
        in_specs=[hbm] * 7,
        out_specs=hbm,
        scratch_shapes=[pltpu.VMEM(*s) for s in scratch] + [pltpu.SMEM((3, NS), jnp.int32), pltpu.SMEM((REC,), jnp.int32)] + semaphores,
        compiler_params=pltpu.CompilerParams(collective_id=0, has_side_effects=True, vmem_limit_bytes=60 << 20),
        name="hyena",
    )(lengths, q, k, v, taps.T, weight, jnp.asarray(dft_tables()))


def solution(mesh):
    two = P("seq", "chan")
    in_specs = (two, two, two, P("chan", "seq"), two, P())
    return jax.shard_map(shards, mesh=mesh, in_specs=in_specs, out_specs=two, check_vma=False)
```

```python
import jax
import jax.numpy as jnp
import numpy as np
from jax import lax
from jax.experimental import pallas as pl
from jax.experimental.pallas import tpu as pltpu
from jax.sharding import PartitionSpec as P

NX, NY, NZ = 4, 4, 8
NS = NY * NZ
BLK = 128
CH = 32
REC = 8
DB = 17
MESH = pl.DeviceIdType.MESH
bf16 = jnp.bfloat16
f32 = jnp.float32
ORDER = [4, 3, 5, 2, 6, 1, 7, 0]
FAR = [2, 1, 3]
CHAINS = [(0, 0), (1, 1), (0, 1), (2, 0), (3, 1), (1, 2), (0, 2), (2, 1), (1, 3), (3, 2), (2, 2), (0, 3), (3, 3), (2, 3)]
FARZ = ["3210", "3210", "2130", "1023", "0123", "0123", "0132", "3021"]


def coords():
    s = lax.axis_index("seq")
    c = lax.axis_index("chan")
    return c // 2, c % 2, s // NZ, s % NZ


def dev(x, core, y, z):
    return (y * NZ + z, x * 2 + core)


def signal(sem, device):
    pl.semaphore_signal(sem, inc=1, device_id=device, device_id_type=MESH)


def remote(src, dst, send, recv, device):
    return pltpu.make_async_remote_copy(
        src_ref=src, dst_ref=dst, send_sem=send, recv_sem=recv, device_id=device, device_id_type=MESH
    )


def dot(a, b):
    return jnp.dot(a, b, preferred_element_type=f32)


class Ring:
    def __init__(self, wt, base, send, recv, x, core, y, z):
        self.wt, self.base, self.send, self.recv, self.y = wt, base, send, recv, y
        self.up = dev(x, core, (y + 1) % NY, z)
        self.down = dev(x, core, (y + NY - 1) % NY, z)

    def copy(self, slot, part, k, device):
        ref = self.wt.at[pl.ds(self.base + part * 256, 256), pl.ds(pl.multiple_of(slot * 256, 256), 256)]
        return remote(ref, ref, self.send.at[k], self.recv.at[k], device)

    def first(self):
        y = self.y
        return [
            self.copy(y, 0, 0, self.up),
            self.copy(y, 1, 1, self.down),
            self.copy(y, 1, 2, self.up),
            self.copy(y, 0, 3, self.down),
        ]

    def forward(self):
        y = self.y
        return [
            self.copy((y + NY - 1) % NY, 0, 4, self.up),
            self.copy((y + 1) % NY, 1, 5, self.down),
        ]

    def start(self, part):
        for c in self.first()[2 * part : 2 * part + 2]:
            c.start()

    def pass_on(self):
        first, forward = self.first(), self.forward()
        for k in range(2):
            first[k].wait_recv()
            forward[k].start()

    def finish_recv(self):
        for c in self.first()[2:] + self.forward():
            c.wait_recv()

    def finish_send(self):
        for c in self.first() + self.forward():
            c.wait_send()


def hyena_kernel(
    len_hbm, q_hbm, k_hbm, v_hbm, t_hbm, w_hbm, tab_hbm, out,
    q_ref, k_ref, v_ref, t_ref, w_ref, tab_ref, tab, tx, rx, qt, qall, hcat, xh, gh, yh, ye, cv, wt, gall, sbuf, rbuf, result, seg, len_ref,
    isem, ssem, rsem, qsend, qrecv, nsem, asend, arecv, bsend, brecv, csend, crecv, w0send, w0recv, w1send, w1recv,
    zsend, zrecv, osem,
):
    x, core, y, z = coords()
    own = (z // 4 == core).astype(jnp.int32)
    mate = dev(x, 1 - core, y, z)
    ys = [dev(x, core, (y + i) % NY, z) for i in FAR]
    xs = [dev((x + i) % NX, core, y, z) for i in FAR]
    zs = [dev(x, core, y, (z + 1) % NZ), dev(x, core, y, (z + NZ - 1) % NZ)]
    barrier = pltpu.get_barrier_semaphore()

    @pl.loop(0, NS)
    def _(i):
        far = dev(x, z // 4, (y + 2 + i // NZ) % NY, (z + 4 + i % NZ) % NZ)

        @pl.when(jnp.logical_not((own == 1) & (i == 2 * NZ + 4)))
        def _():
            signal(barrier, far)

    for d in ys + xs + zs + [mate]:
        signal(barrier, d)

    loads = [
        pltpu.make_async_copy(src, dst, isem.at[i])
        for i, (src, dst) in enumerate(
            [(k_hbm, k_ref), (v_hbm, v_ref), (t_hbm, t_ref), (w_hbm, w_ref), (q_hbm, q_ref), (tab_hbm, tab_ref), (len_hbm, len_ref)]
        )
    ]
    for c in loads:
        c.start()

    def flip(a):
        return a.T

    loads[0].wait()
    loads[1].wait()
    for c in range(8):
        cols = pl.ds(c * BLK, BLK)
        prod = (k_ref[:, cols].astype(f32) * v_ref[:, cols].astype(f32)).astype(bf16)
        tx[pl.ds(4 * c, 4), pl.ds(0, CH), :] = flip(prod).reshape(4, CH, BLK)
    loads[2].wait()
    for c in range(8):
        taps = t_ref[:, pl.ds(c * BLK, BLK)].T.reshape(4, CH, 64)
        taps = jnp.concatenate([taps[:, :16], taps[:, 16:]], axis=2)
        tx[pl.ds(4 * c, 4), pl.ds(CH, 16), :] = taps.astype(bf16)

    pl.semaphore_wait(barrier, NS - own + 9)

    def chunk(i):
        return (i + 2 * (z % 4) + core) % 8

    def piece(i):
        c = chunk(i // 4)
        yy = (y + (6 - i % 4) % 4) % NY
        to = dev(x, c % 2, yy, 4 * core + c // 2)
        here = (own == 1) & (c == 2 * (z % 4) + core) & (yy == y)
        return here, 4 * c + yy, to

    def post(i, src, dst, send, recv):
        here, p, to = piece(i)

        @pl.when(here)
        def _():
            pltpu.make_async_copy(src.at[p], dst.at[y * NZ + z], recv).start()

        @pl.when(jnp.logical_not(here))
        def _():
            remote(src.at[p], dst.at[y * NZ + z], send.at[i], recv, to).start()

    def posted(i, src, dst, send, recv):
        here, p, to = piece(i)

        @pl.when(jnp.logical_not(here))
        def _():
            remote(src.at[p], dst.at[y * NZ + z], send.at[i], recv, to).wait_send()

    @pl.loop(0, NS)
    def _(i):
        post(i, tx, rx, ssem, rsem)

    loads[4].wait()
    for c in range(8):
        qt[c] = flip(q_ref[:, pl.ds(c * BLK, BLK)])
    farz = jnp.int32(0)
    for i, digits in enumerate(FARZ):
        farz = jnp.where((4 * core + 8 - z) % 8 == i, int(digits[::-1], 4), farz)

    def q_piece(i):
        digit = farz
        for k in range(1, 4):
            digit = jnp.where(i // 2 == k, farz // 4**k, digit)
        p = 2 * (digit % 4) + (i + core) % 2
        to = dev(x, p % 2, y, 4 * core + p // 2)
        here = (own == 1) & (p == 2 * (z % 4) + core)
        return here, qt.at[p], qall.at[z], to

    def q_post(low, high):
        @pl.loop(low, high)
        def _(i):
            here, src, dst, to = q_piece(i)

            @pl.when(here)
            def _():
                pltpu.make_async_copy(src, dst, qrecv.at[z]).start()

            @pl.when(jnp.logical_not(here))
            def _():
                remote(src, dst, qsend.at[i], qrecv.at[z], to).start()

    q_post(0, 2)

    loads[3].wait()
    w_cols = pl.ds(pl.multiple_of(y * 256, 256), 256)
    for c in range(4):
        wt[pl.ds(c * BLK, BLK), w_cols] = flip(w_ref[:, pl.ds(c * BLK, BLK)])
    rings = [Ring(wt, 0, w0send, w0recv, x, core, y, z), Ring(wt, 512, w1send, w1recv, x, core, y, z)]
    rings[0].start(0)
    rings[0].start(1)


    for c in range(4):
        wt[pl.ds(512 + c * BLK, BLK), w_cols] = flip(w_ref[:, pl.ds(512 + c * BLK, BLK)])

    loads[6].wait()
    bounds = []
    begin = jnp.int32(0)
    for r in range(REC):
        bounds.append((begin, begin + len_ref[r]))
        begin = begin + len_ref[r]

    @pl.loop(0, NS)
    def _(n):
        t = n * BLK
        first, last, extra = bounds[0][0], bounds[0][1], jnp.int32(NS)
        for r in range(1, REC):
            past = bounds[r][0] <= t
            first = jnp.where(past, bounds[r][0], first)
            last = jnp.where(past, bounds[r][1], last)
            extra = jnp.where(past, NS + r, extra)
        block = first // BLK
        seg[0, n] = block
        seg[1, n] = last
        seg[2, n] = jnp.where(first == block * BLK, block, extra)

    loads[5].wait()
    for i, cols in enumerate((pl.ds(0, 2 * BLK), pl.ds(2 * BLK, BLK))):
        table = tab_ref[:, cols]
        hi = table.astype(bf16)
        lo = (table - hi.astype(f32)).astype(bf16)
        if i == 0:
            tab[0], tab[1] = hi, lo
            tab[2] = jnp.concatenate([hi[:BLK], lo[:BLK]], axis=0)
        else:
            tab[3] = jnp.concatenate([hi, lo], axis=1)
    rings[0].pass_on()
    rings[1].start(0)
    pltpu.make_async_copy(tx, rx, rsem).wait()
    q_post(2, 8)

    lane16 = lax.broadcasted_iota(jnp.int32, (16, BLK), 1)
    lane = lax.broadcasted_iota(jnp.int32, (CH, BLK), 1)
    zero = jnp.zeros((CH, BLK), bf16)
    hcat[0, :, pl.ds(BLK, BLK)] = zero
    hcat[DB - 1, :, pl.ds(0, BLK)] = zero

    for d in range(DB - 1):
        a = rx[2 * d, pl.ds(CH, 16), :].astype(f32)
        b = rx[2 * d + 1, pl.ds(CH, 16), :].astype(f32)
        top = jnp.where(lane16 < 64, a, pltpu.roll(b, 64, 1))
        bottom = jnp.where(lane16 < 64, pltpu.roll(a, 64, 1), b)
        h = jnp.concatenate([top, bottom], axis=0).astype(bf16)
        hcat[d, :, pl.ds(0, BLK)] = h
        hcat[d + 1, :, pl.ds(BLK, BLK)] = h

    def row(n):
        if n < NS:
            value = rx[n, pl.ds(0, CH), :].astype(f32)
            return jnp.where(lane + n * BLK < seg[1, n], value, 0.0).astype(bf16)
        if n == NS:
            return zero
        begin, end = bounds[n - NS]
        m = begin // BLK
        token = lane + m * BLK
        value = rx[m, pl.ds(0, CH), :].astype(f32)
        return jnp.where((token >= begin) & (token < end), value, 0.0).astype(bf16)

    for g in range(5):
        rows = jnp.concatenate([row(8 * g + n) for n in range(8)], axis=0)
        spectrum = dot(jnp.concatenate([rows, rows], axis=1), tab[2])
        xh[pl.ds(8 * g, 8)] = spectrum.reshape(8, CH, 2 * BLK)

    for lo, size in ((0, 8), (8, 9)):
        taps = hcat[pl.ds(lo, size)].reshape(size * CH, 2 * BLK)
        gh[pl.ds(lo, size)] = (dot(taps, tab[0]) + dot(taps, tab[1])).reshape(size, CH, 2 * BLK)

    re, im = pl.ds(0, BLK), pl.ds(BLK, BLK)

    def inverse(rows):
        hi = rows.astype(bf16)
        lo = (rows - hi.astype(f32)).astype(bf16)
        both = dot(hi, tab[3])
        return both[:, :BLK] + both[:, BLK:] + dot(lo, tab[3, :, :BLK])

    gr, gi = gh[0, :, re], gh[0, :, im]
    for r in range(REC):
        xr, xi = xh[NS + r, :, re], xh[NS + r, :, im]
        ye[r, :, re] = xr * gr - xi * gi
        ye[r, :, im] = xr * gi + xi * gr
    ye[:, :, re] = inverse(ye[...].reshape(REC * CH, 2 * BLK)).reshape(REC, CH, BLK)

    def place(rel):
        return (z + rel) % NZ

    def convolve(rel):
        b = place(rel)

        @pl.loop(0, NY, unroll=4)
        def _(j):
            n = j * NZ + b
            block, first = seg[0, n], seg[2, n]
            acc_re = jnp.zeros((CH, BLK), f32)
            acc_im = jnp.zeros((CH, BLK), f32)
            for d in range(DB):
                m = n - d
                row = jnp.where(m > block, m, jnp.where(m == block, first, NS))
                xr, xi = xh[row, :, re], xh[row, :, im]
                gr, gi = gh[d, :, re], gh[d, :, im]
                acc_re = acc_re + (xr * gr - xi * gi)
                acc_im = acc_im + (xr * gi + xi * gr)
            yh[j, :, re] = acc_re
            yh[j, :, im] = acc_im

        back = inverse(yh[...].reshape(NY * CH, 2 * BLK)).reshape(NY, CH, BLK)
        for j in range(NY):
            n = j * NZ + b
            token = lane + n * BLK
            value = back[j]
            for r in range(1, REC):
                begin, end = bounds[r]
                low = jnp.where(begin > n * BLK, begin, TOKENS_END)
                value = jnp.where((token >= low) & (token < end), ye[r, :, re], value)
            cv[rel, j] = value.astype(bf16)

    def a_dst(rel):
        return gall.at[place(rel), x, core, pl.ds(CH * y, CH)]

    def a_near(rel):
        return pltpu.make_async_copy(cv.at[rel, y], a_dst(rel), arecv.at[rel])

    def a_far(rel):
        return [
            remote(cv.at[rel, (y + i) % NY], a_dst(rel), asend.at[rel, i], arecv.at[rel], d)
            for i, d in zip(FAR, ys)
        ]

    def b_copies(rel):
        ref = gall.at[place(rel), x, core]
        return [remote(ref, ref, bsend.at[rel, i], brecv.at[rel, i], d) for i, d in enumerate(xs)]

    def c_copy(rel):
        ref = gall.at[place(rel), :, core]
        return remote(ref, ref, csend.at[rel], crecv.at[rel], mate)

    def conv(i):
        rel = ORDER[i]
        convolve(rel)
        for c in a_far(rel):
            c.start()
        a_near(rel).start()

    def spread(i):
        rel = ORDER[i]
        b = place(rel)
        ref = gall.at[b, x, core]
        pltpu.make_async_copy(ref, ref, arecv.at[rel]).wait()
        pltpu.make_async_copy(qall.at[b], qall.at[b], qrecv.at[b]).wait()
        gall[b, x, core] = (gall[b, x, core].astype(f32) * qall[b].astype(f32)).astype(bf16)
        for c in b_copies(rel):
            c.start()

    def share(i):
        rel = ORDER[i]
        for c in b_copies(rel):
            c.wait_recv()
        c_copy(rel).start()

    def ready(i):
        c_copy(ORDER[i]).wait_recv()

    def z_copy(way, h, step):
        return remote(
            sbuf.at[way, h, step], rbuf.at[way, h, step], zsend.at[way, h, step], zrecv.at[way, h, step], zs[way]
        )

    def sends(way, h, step):
        return step < 4 and (step > 0 or way == h % 2)

    def rows(h):
        return pl.ds(256 * h, 256)

    def term(h, rel):
        return dot(wt[rows(h), :], gall[place(rel)].reshape(1024, BLK))

    def ring_send(h, step):
        for way in range(2):
            k = h ^ way
            total = term(k, 4 - step if way == 0 else 4 + step)
            if step > 0 and sends(way, k, step - 1):
                z_copy(way, k, step - 1).wait_recv()
                total = total + rbuf[way, k, step - 1].astype(f32)
            sbuf[way, k, step] = total.astype(bf16)
            z_copy(way, k, step).start()

    def store(h):
        return pltpu.make_async_copy(result.at[:, rows(h)], out.at[:, rows(h)], osem.at[h])

    def ring_end():
        terms = [term(h, 0) for h in range(4)]
        for h in (0, 1, 2, 3):
            total = terms[h]
            for way in range(2):
                z_copy(way, h, 3).wait_recv()
                total = total + rbuf[way, h, 3].astype(f32)
            result[:, rows(h)] = total.T.astype(bf16)
            store(h).start()

    for i in range(4):
        conv(i)
        if i == 2:
            rings[1].start(1)
    for i in range(4):
        if i < 3:
            spread(i)
        conv(4 + i)
    rings[1].pass_on()
    rings[0].finish_recv()
    before = {
        0: ((), (0,), (0,)),
        1: ((3,), (1, 2), (1, 2)),
        2: ((4, 5), (), ()),
        3: ((6,), (), ()),
        4: ((7,), (3, 4), ()),
        5: ((), (), (3, 4)),
        7: ((), (5, 6), ()),
        8: ((), (), (5, 6)),
        11: ((), (7,), ()),
    }
    for i, (h, step) in enumerate(CHAINS):
        if i == 3:
            rings[1].finish_recv()
        spreads, shares, needs = before.get(i, ((), (), ()))
        for k in spreads:
            spread(k)
        for k in shares:
            share(k)
        for k in needs:
            ready(k)
        ring_send(h, step)
    ready(7)
    ring_end()

    @pl.loop(0, NS)
    def _(i):
        posted(i, tx, rx, ssem, rsem)

    @pl.loop(0, 8)
    def _(i):
        here, src, dst, to = q_piece(i)

        @pl.when(jnp.logical_not(here))
        def _():
            remote(src, dst, qsend.at[i], qrecv.at[z], to).wait_send()

    for rel in range(NZ):
        for c in a_far(rel) + b_copies(rel) + [c_copy(rel)]:
            c.wait_send()
    for way in range(2):
        for h in range(4):
            for step in range(4):
                if sends(way, h, step):
                    z_copy(way, h, step).wait_send()
    for ring in rings:
        ring.finish_send()
    for h in range(4):
        store(h).wait()


TOKENS_END = NS * BLK


def dft_tables():
    theta = 2.0 * np.pi * (np.arange(BLK) + 0.5) / (2 * BLK)
    angle = np.arange(2 * BLK)[:, None] * theta[None, :]
    sign = np.where(np.arange(2 * BLK) < BLK, 1.0, -1.0)[:, None]
    forward = sign * np.concatenate([np.cos(angle), -np.sin(angle)], axis=1)
    angle = theta[:, None] * np.arange(BLK)[None, :]
    inverse = np.concatenate([np.cos(angle), -np.sin(angle)], axis=0) / BLK
    return np.concatenate([forward, inverse], axis=1).astype(np.float32)


def shards(q, k, v, taps, weight, lengths):
    hbm = pl.BlockSpec(memory_space=pl.ANY)
    dma = pltpu.SemaphoreType.DMA
    scratch = [
        ((BLK, 1024), bf16),
        ((BLK, 1024), bf16),
        ((BLK, 1024), bf16),
        ((64, 1024), f32),
        ((256, 1024), bf16),
        ((256, 384), f32),
        ((4, 256, 256), bf16),
        ((NS, 48, BLK), bf16),
        ((NS, 48, BLK), bf16),
        ((8, BLK, BLK), bf16),
        ((8, BLK, BLK), bf16),
        ((DB, CH, 2 * BLK), bf16),
        ((NS + REC, CH, 2 * BLK), f32),
        ((DB, CH, 2 * BLK), f32),
        ((NY, CH, 2 * BLK), f32),
        ((REC, CH, 2 * BLK), f32),
        ((NZ, NY, CH, BLK), bf16),
        ((1024, 1024), bf16),
        ((NZ, NX, 2, BLK, BLK), bf16),
        ((2, 4, 4, 256, BLK), bf16),
        ((2, 4, 4, 256, BLK), bf16),
        ((BLK, 1024), bf16),
    ]
    semaphores = [
        dma((7,)), dma((NS,)), dma, dma((8,)), dma((NZ,)), dma, dma((NZ, NY)), dma((NZ,)), dma((NZ, NX)), dma((NZ, NX)),
        dma((NZ,)), dma((NZ,)), dma((6,)), dma((6,)), dma((6,)), dma((6,)), dma((2, 4, 4)), dma((2, 4, 4)), dma((4,)),
    ]
    return pl.pallas_call(
        hyena_kernel,
        out_shape=jax.ShapeDtypeStruct((BLK, 1024), bf16),
        in_specs=[hbm] * 7,
        out_specs=hbm,
        scratch_shapes=[pltpu.VMEM(*s) for s in scratch] + [pltpu.SMEM((3, NS), jnp.int32), pltpu.SMEM((REC,), jnp.int32)] + semaphores,
        compiler_params=pltpu.CompilerParams(collective_id=0, has_side_effects=True, vmem_limit_bytes=60 << 20),
        name="hyena",
    )(lengths, q, k, v, taps.T, weight, jnp.asarray(dft_tables()))


def solution(mesh):
    two = P("seq", "chan")
    in_specs = (two, two, two, P("chan", "seq"), two, P())
    return jax.shard_map(shards, mesh=mesh, in_specs=in_specs, out_specs=two, check_vma=False)
```

```python
import jax
import jax.numpy as jnp
import numpy as np
from jax import lax
from jax.experimental import pallas as pl
from jax.experimental.pallas import tpu as pltpu
from jax.sharding import PartitionSpec as P

NX, NY, NZ = 4, 4, 8
NS = NY * NZ
BLK = 128
CH = 32
REC = 8
DB = 17
MESH = pl.DeviceIdType.MESH
bf16 = jnp.bfloat16
f32 = jnp.float32
ORDER = [4, 3, 5, 2, 6, 1, 7, 0]
FAR = [2, 1, 3]
CHAINS = [(0, 0), (1, 1), (0, 1), (2, 0), (3, 1), (1, 2), (0, 2), (2, 1), (1, 3), (3, 2), (2, 2), (0, 3), (3, 3), (2, 3)]
FARZ = ["3210", "3210", "2130", "1023", "0123", "0123", "0132", "3021"]


def coords():
    s = lax.axis_index("seq")
    c = lax.axis_index("chan")
    return c // 2, c % 2, s // NZ, s % NZ


def dev(x, core, y, z):
    return (y * NZ + z, x * 2 + core)


def signal(sem, device):
    pl.semaphore_signal(sem, inc=1, device_id=device, device_id_type=MESH)


def remote(src, dst, send, recv, device):
    return pltpu.make_async_remote_copy(
        src_ref=src, dst_ref=dst, send_sem=send, recv_sem=recv, device_id=device, device_id_type=MESH
    )


def dot(a, b):
    return jnp.dot(a, b, preferred_element_type=f32)


class Ring:
    def __init__(self, wt, base, send, recv, x, core, y, z):
        self.wt, self.base, self.send, self.recv, self.y = wt, base, send, recv, y
        self.up = dev(x, core, (y + 1) % NY, z)
        self.down = dev(x, core, (y + NY - 1) % NY, z)

    def copy(self, slot, part, k, device):
        ref = self.wt.at[pl.ds(self.base + part * 256, 256), pl.ds(pl.multiple_of(slot * 256, 256), 256)]
        return remote(ref, ref, self.send.at[k], self.recv.at[k], device)

    def first(self):
        y = self.y
        return [
            self.copy(y, 0, 0, self.up),
            self.copy(y, 1, 1, self.down),
            self.copy(y, 1, 2, self.up),
            self.copy(y, 0, 3, self.down),
        ]

    def forward(self):
        y = self.y
        return [
            self.copy((y + NY - 1) % NY, 0, 4, self.up),
            self.copy((y + 1) % NY, 1, 5, self.down),
        ]

    def start(self, part):
        for c in self.first()[2 * part : 2 * part + 2]:
            c.start()

    def pass_on(self):
        first, forward = self.first(), self.forward()
        for k in range(2):
            first[k].wait_recv()
            forward[k].start()

    def finish_recv(self):
        for c in self.first()[2:] + self.forward():
            c.wait_recv()

    def finish_send(self):
        for c in self.first() + self.forward():
            c.wait_send()


def hyena_kernel(
    len_hbm, q_hbm, k_hbm, v_hbm, t_hbm, w_hbm, tab_hbm, out,
    q_ref, k_ref, v_ref, t_ref, w_ref, tab_ref, tab, tx, rx, qt, qall, hcat, xh, gh, yh, ye, cv, wt, gall, sbuf, rbuf, result, seg, len_ref,
    isem, ssem, rsem, qsend, qrecv, nsem, asend, arecv, bsend, brecv, csend, crecv, w0send, w0recv, w1send, w1recv,
    zsend, zrecv, osem,
):
    x, core, y, z = coords()
    own = (z // 4 == core).astype(jnp.int32)
    mate = dev(x, 1 - core, y, z)
    ys = [dev(x, core, (y + i) % NY, z) for i in FAR]
    xs = [dev((x + i) % NX, core, y, z) for i in FAR]
    zs = [dev(x, core, y, (z + 1) % NZ), dev(x, core, y, (z + NZ - 1) % NZ)]
    barrier = pltpu.get_barrier_semaphore()

    @pl.loop(0, NS)
    def _(i):
        far = dev(x, z // 4, (y + 2 + i // NZ) % NY, (z + 4 + i % NZ) % NZ)

        @pl.when(jnp.logical_not((own == 1) & (i == 2 * NZ + 4)))
        def _():
            signal(barrier, far)

    for d in ys + xs + zs + [mate]:
        signal(barrier, d)

    loads = [
        pltpu.make_async_copy(src, dst, isem.at[i])
        for i, (src, dst) in enumerate(
            [(k_hbm, k_ref), (v_hbm, v_ref), (t_hbm, t_ref), (w_hbm, w_ref), (q_hbm, q_ref), (tab_hbm, tab_ref), (len_hbm, len_ref)]
        )
    ]
    for c in loads:
        c.start()

    def flip(a):
        return a.T

    loads[0].wait()
    loads[1].wait()
    for c in range(8):
        cols = pl.ds(c * BLK, BLK)
        prod = (k_ref[:, cols].astype(f32) * v_ref[:, cols].astype(f32)).astype(bf16)
        tx[pl.ds(4 * c, 4), pl.ds(0, CH), :] = flip(prod).reshape(4, CH, BLK)
    loads[2].wait()
    for c in range(8):
        taps = t_ref[:, pl.ds(c * BLK, BLK)].T.reshape(4, CH, 64)
        taps = jnp.concatenate([taps[:, :16], taps[:, 16:]], axis=2)
        tx[pl.ds(4 * c, 4), pl.ds(CH, 16), :] = taps.astype(bf16)

    pl.semaphore_wait(barrier, NS - own + 9)

    def chunk(i):
        return (i + 2 * (z % 4) + core) % 8

    def piece(i):
        c = chunk(i // 4)
        yy = (y + (6 - i % 4) % 4) % NY
        to = dev(x, c % 2, yy, 4 * core + c // 2)
        here = (own == 1) & (c == 2 * (z % 4) + core) & (yy == y)
        return here, 4 * c + yy, to

    def post(i, src, dst, send, recv):
        here, p, to = piece(i)

        @pl.when(here)
        def _():
            pltpu.make_async_copy(src.at[p], dst.at[y * NZ + z], recv).start()

        @pl.when(jnp.logical_not(here))
        def _():
            remote(src.at[p], dst.at[y * NZ + z], send.at[i], recv, to).start()

    def posted(i, src, dst, send, recv):
        here, p, to = piece(i)

        @pl.when(jnp.logical_not(here))
        def _():
            remote(src.at[p], dst.at[y * NZ + z], send.at[i], recv, to).wait_send()

    @pl.loop(0, NS)
    def _(i):
        post(i, tx, rx, ssem, rsem)

    loads[4].wait()
    for c in range(8):
        qt[c] = flip(q_ref[:, pl.ds(c * BLK, BLK)])
    farz = jnp.int32(0)
    for i, digits in enumerate(FARZ):
        farz = jnp.where((4 * core + 8 - z) % 8 == i, int(digits[::-1], 4), farz)

    def q_piece(i):
        digit = farz
        for k in range(1, 4):
            digit = jnp.where(i // 2 == k, farz // 4**k, digit)
        p = 2 * (digit % 4) + (i + core) % 2
        to = dev(x, p % 2, y, 4 * core + p // 2)
        here = (own == 1) & (p == 2 * (z % 4) + core)
        return here, qt.at[p], qall.at[z], to

    def q_post(low, high):
        @pl.loop(low, high)
        def _(i):
            here, src, dst, to = q_piece(i)

            @pl.when(here)
            def _():
                pltpu.make_async_copy(src, dst, qrecv.at[z]).start()

            @pl.when(jnp.logical_not(here))
            def _():
                remote(src, dst, qsend.at[i], qrecv.at[z], to).start()

    q_post(0, 2)

    loads[3].wait()
    w_cols = pl.ds(pl.multiple_of(y * 256, 256), 256)
    for c in range(4):
        wt[pl.ds(c * BLK, BLK), w_cols] = flip(w_ref[:, pl.ds(c * BLK, BLK)])
    rings = [Ring(wt, 0, w0send, w0recv, x, core, y, z), Ring(wt, 512, w1send, w1recv, x, core, y, z)]
    rings[0].start(0)
    rings[0].start(1)


    for c in range(4):
        wt[pl.ds(512 + c * BLK, BLK), w_cols] = flip(w_ref[:, pl.ds(512 + c * BLK, BLK)])

    loads[6].wait()
    bounds = []
    begin = jnp.int32(0)
    for r in range(REC):
        bounds.append((begin, begin + len_ref[r]))
        begin = begin + len_ref[r]

    @pl.loop(0, NS)
    def _(n):
        t = n * BLK
        first, last, extra = bounds[0][0], bounds[0][1], jnp.int32(NS)
        for r in range(1, REC):
            past = bounds[r][0] <= t
            first = jnp.where(past, bounds[r][0], first)
            last = jnp.where(past, bounds[r][1], last)
            extra = jnp.where(past, NS + r, extra)
        block = first // BLK
        seg[0, n] = block
        seg[1, n] = last
        seg[2, n] = jnp.where(first == block * BLK, block, extra)

    loads[5].wait()
    for i, cols in enumerate((pl.ds(0, 2 * BLK), pl.ds(2 * BLK, BLK))):
        table = tab_ref[:, cols]
        hi = table.astype(bf16)
        lo = (table - hi.astype(f32)).astype(bf16)
        if i == 0:
            tab[0], tab[1] = hi, lo
            tab[2] = jnp.concatenate([hi[:BLK], lo[:BLK]], axis=0)
        else:
            tab[3] = jnp.concatenate([hi, lo], axis=1)
    rings[0].pass_on()
    rings[1].start(0)
    pltpu.make_async_copy(tx, rx, rsem).wait()

    lane16 = lax.broadcasted_iota(jnp.int32, (16, BLK), 1)
    lane = lax.broadcasted_iota(jnp.int32, (CH, BLK), 1)
    zero = jnp.zeros((CH, BLK), bf16)
    hcat[0, :, pl.ds(BLK, BLK)] = zero
    hcat[DB - 1, :, pl.ds(0, BLK)] = zero

    for d in range(DB - 1):
        a = rx[2 * d, pl.ds(CH, 16), :].astype(f32)
        b = rx[2 * d + 1, pl.ds(CH, 16), :].astype(f32)
        top = jnp.where(lane16 < 64, a, pltpu.roll(b, 64, 1))
        bottom = jnp.where(lane16 < 64, pltpu.roll(a, 64, 1), b)
        h = jnp.concatenate([top, bottom], axis=0).astype(bf16)
        hcat[d, :, pl.ds(0, BLK)] = h
        hcat[d + 1, :, pl.ds(BLK, BLK)] = h

    def row(n):
        if n < NS:
            value = rx[n, pl.ds(0, CH), :].astype(f32)
            return jnp.where(lane + n * BLK < seg[1, n], value, 0.0).astype(bf16)
        if n == NS:
            return zero
        begin, end = bounds[n - NS]
        m = begin // BLK
        token = lane + m * BLK
        value = rx[m, pl.ds(0, CH), :].astype(f32)
        return jnp.where((token >= begin) & (token < end), value, 0.0).astype(bf16)

    for g in range(5):
        rows = jnp.concatenate([row(8 * g + n) for n in range(8)], axis=0)
        spectrum = dot(jnp.concatenate([rows, rows], axis=1), tab[2])
        xh[pl.ds(8 * g, 8)] = spectrum.reshape(8, CH, 2 * BLK)

    for lo, size in ((0, 8), (8, 9)):
        taps = hcat[pl.ds(lo, size)].reshape(size * CH, 2 * BLK)
        gh[pl.ds(lo, size)] = (dot(taps, tab[0]) + dot(taps, tab[1])).reshape(size, CH, 2 * BLK)

    re, im = pl.ds(0, BLK), pl.ds(BLK, BLK)

    def inverse(rows):
        hi = rows.astype(bf16)
        lo = (rows - hi.astype(f32)).astype(bf16)
        both = dot(hi, tab[3])
        return both[:, :BLK] + both[:, BLK:] + dot(lo, tab[3, :, :BLK])

    gr, gi = gh[0, :, re], gh[0, :, im]
    for r in range(REC):
        xr, xi = xh[NS + r, :, re], xh[NS + r, :, im]
        ye[r, :, re] = xr * gr - xi * gi
        ye[r, :, im] = xr * gi + xi * gr
    ye[:, :, re] = inverse(ye[...].reshape(REC * CH, 2 * BLK)).reshape(REC, CH, BLK)

    def place(rel):
        return (z + rel) % NZ

    def convolve(rel):
        b = place(rel)

        @pl.loop(0, NY, unroll=4)
        def _(j):
            n = j * NZ + b
            block, first = seg[0, n], seg[2, n]
            acc_re = jnp.zeros((CH, BLK), f32)
            acc_im = jnp.zeros((CH, BLK), f32)
            for d in range(DB):
                m = n - d
                row = jnp.where(m > block, m, jnp.where(m == block, first, NS))
                xr, xi = xh[row, :, re], xh[row, :, im]
                gr, gi = gh[d, :, re], gh[d, :, im]
                acc_re = acc_re + (xr * gr - xi * gi)
                acc_im = acc_im + (xr * gi + xi * gr)
            yh[j, :, re] = acc_re
            yh[j, :, im] = acc_im

        back = inverse(yh[...].reshape(NY * CH, 2 * BLK)).reshape(NY, CH, BLK)
        for j in range(NY):
            n = j * NZ + b
            token = lane + n * BLK
            value = back[j]
            for r in range(1, REC):
                begin, end = bounds[r]
                low = jnp.where(begin > n * BLK, begin, TOKENS_END)
                value = jnp.where((token >= low) & (token < end), ye[r, :, re], value)
            cv[rel, j] = value.astype(bf16)

    def a_dst(rel):
        return gall.at[place(rel), x, core, pl.ds(CH * y, CH)]

    def a_near(rel):
        return pltpu.make_async_copy(cv.at[rel, y], a_dst(rel), arecv.at[rel])

    def a_far(rel):
        return [
            remote(cv.at[rel, (y + i) % NY], a_dst(rel), asend.at[rel, i], arecv.at[rel], d)
            for i, d in zip(FAR, ys)
        ]

    def b_copies(rel):
        ref = gall.at[place(rel), x, core]
        return [remote(ref, ref, bsend.at[rel, i], brecv.at[rel, i], d) for i, d in enumerate(xs)]

    def c_copy(rel):
        ref = gall.at[place(rel), :, core]
        return remote(ref, ref, csend.at[rel], crecv.at[rel], mate)

    def conv(i):
        rel = ORDER[i]
        convolve(rel)
        for c in a_far(rel):
            c.start()
        a_near(rel).start()

    def spread(i):
        rel = ORDER[i]
        b = place(rel)
        ref = gall.at[b, x, core]
        pltpu.make_async_copy(ref, ref, arecv.at[rel]).wait()
        pltpu.make_async_copy(qall.at[b], qall.at[b], qrecv.at[b]).wait()
        gall[b, x, core] = (gall[b, x, core].astype(f32) * qall[b].astype(f32)).astype(bf16)
        for c in b_copies(rel):
            c.start()

    def share(i):
        rel = ORDER[i]
        for c in b_copies(rel):
            c.wait_recv()
        c_copy(rel).start()

    def ready(i):
        c_copy(ORDER[i]).wait_recv()

    def z_copy(way, h, step):
        return remote(
            sbuf.at[way, h, step], rbuf.at[way, h, step], zsend.at[way, h, step], zrecv.at[way, h, step], zs[way]
        )

    def sends(way, h, step):
        return step < 4 and (step > 0 or way == h % 2)

    def rows(h):
        return pl.ds(256 * h, 256)

    def term(h, rel):
        return dot(wt[rows(h), :], gall[place(rel)].reshape(1024, BLK))

    def ring_send(h, step):
        for way in range(2):
            k = h ^ way
            total = term(k, 4 - step if way == 0 else 4 + step)
            if step > 0 and sends(way, k, step - 1):
                z_copy(way, k, step - 1).wait_recv()
                total = total + rbuf[way, k, step - 1].astype(f32)
            sbuf[way, k, step] = total.astype(bf16)
            z_copy(way, k, step).start()

    def store(h):
        return pltpu.make_async_copy(result.at[:, rows(h)], out.at[:, rows(h)], osem.at[h])

    def ring_end():
        terms = [term(h, 0) for h in range(4)]
        for h in (0, 1, 2, 3):
            total = terms[h]
            for way in range(2):
                z_copy(way, h, 3).wait_recv()
                total = total + rbuf[way, h, 3].astype(f32)
            result[:, rows(h)] = total.T.astype(bf16)
            store(h).start()

    for i in range(4):
        conv(i)
        if i == 0:
            q_post(2, 8)
        if i == 2:
            rings[1].start(1)
    for i in range(4):
        if i < 3:
            spread(i)
        conv(4 + i)
    rings[1].pass_on()
    rings[0].finish_recv()
    before = {
        0: ((), (0,), (0,)),
        1: ((3,), (1, 2), (1, 2)),
        2: ((4, 5), (), ()),
        3: ((6,), (), ()),
        4: ((7,), (3, 4), ()),
        5: ((), (), (3, 4)),
        7: ((), (5, 6), ()),
        8: ((), (), (5, 6)),
        11: ((), (7,), ()),
    }
    for i, (h, step) in enumerate(CHAINS):
        if i == 3:
            rings[1].finish_recv()
        spreads, shares, needs = before.get(i, ((), (), ()))
        for k in spreads:
            spread(k)
        for k in shares:
            share(k)
        for k in needs:
            ready(k)
        ring_send(h, step)
    ready(7)
    ring_end()

    @pl.loop(0, NS)
    def _(i):
        posted(i, tx, rx, ssem, rsem)

    @pl.loop(0, 8)
    def _(i):
        here, src, dst, to = q_piece(i)

        @pl.when(jnp.logical_not(here))
        def _():
            remote(src, dst, qsend.at[i], qrecv.at[z], to).wait_send()

    for rel in range(NZ):
        for c in a_far(rel) + b_copies(rel) + [c_copy(rel)]:
            c.wait_send()
    for way in range(2):
        for h in range(4):
            for step in range(4):
                if sends(way, h, step):
                    z_copy(way, h, step).wait_send()
    for ring in rings:
        ring.finish_send()
    for h in range(4):
        store(h).wait()


TOKENS_END = NS * BLK


def dft_tables():
    theta = 2.0 * np.pi * (np.arange(BLK) + 0.5) / (2 * BLK)
    angle = np.arange(2 * BLK)[:, None] * theta[None, :]
    sign = np.where(np.arange(2 * BLK) < BLK, 1.0, -1.0)[:, None]
    forward = sign * np.concatenate([np.cos(angle), -np.sin(angle)], axis=1)
    angle = theta[:, None] * np.arange(BLK)[None, :]
    inverse = np.concatenate([np.cos(angle), -np.sin(angle)], axis=0) / BLK
    return np.concatenate([forward, inverse], axis=1).astype(np.float32)


def shards(q, k, v, taps, weight, lengths):
    hbm = pl.BlockSpec(memory_space=pl.ANY)
    dma = pltpu.SemaphoreType.DMA
    scratch = [
        ((BLK, 1024), bf16),
        ((BLK, 1024), bf16),
        ((BLK, 1024), bf16),
        ((64, 1024), f32),
        ((256, 1024), bf16),
        ((256, 384), f32),
        ((4, 256, 256), bf16),
        ((NS, 48, BLK), bf16),
        ((NS, 48, BLK), bf16),
        ((8, BLK, BLK), bf16),
        ((8, BLK, BLK), bf16),
        ((DB, CH, 2 * BLK), bf16),
        ((NS + REC, CH, 2 * BLK), f32),
        ((DB, CH, 2 * BLK), f32),
        ((NY, CH, 2 * BLK), f32),
        ((REC, CH, 2 * BLK), f32),
        ((NZ, NY, CH, BLK), bf16),
        ((1024, 1024), bf16),
        ((NZ, NX, 2, BLK, BLK), bf16),
        ((2, 4, 4, 256, BLK), bf16),
        ((2, 4, 4, 256, BLK), bf16),
        ((BLK, 1024), bf16),
    ]
    semaphores = [
        dma((7,)), dma((NS,)), dma, dma((8,)), dma((NZ,)), dma, dma((NZ, NY)), dma((NZ,)), dma((NZ, NX)), dma((NZ, NX)),
        dma((NZ,)), dma((NZ,)), dma((6,)), dma((6,)), dma((6,)), dma((6,)), dma((2, 4, 4)), dma((2, 4, 4)), dma((4,)),
    ]
    return pl.pallas_call(
        hyena_kernel,
        out_shape=jax.ShapeDtypeStruct((BLK, 1024), bf16),
        in_specs=[hbm] * 7,
        out_specs=hbm,
        scratch_shapes=[pltpu.VMEM(*s) for s in scratch] + [pltpu.SMEM((3, NS), jnp.int32), pltpu.SMEM((REC,), jnp.int32)] + semaphores,
        compiler_params=pltpu.CompilerParams(collective_id=0, has_side_effects=True, vmem_limit_bytes=60 << 20),
        name="hyena",
    )(lengths, q, k, v, taps.T, weight, jnp.asarray(dft_tables()))


def solution(mesh):
    two = P("seq", "chan")
    in_specs = (two, two, two, P("chan", "seq"), two, P())
    return jax.shard_map(shards, mesh=mesh, in_specs=in_specs, out_specs=two, check_vma=False)
```
